1024 devices in a mesh: dp: 32 (over x, y), replica: 32 (over z, core).
Axes of the slice: x: 4, y: 8, z: 16, core: 2. Of those that a mesh axis runs over, the one named last changes fastest.
Arguments:
- grads: bfloat16 [32, 64, 512, 512], P('dp', None, 'replica'), may hold values from -2.5 to 2.5
- assignment: int32 [64, 1], replicated, may hold values from 0 to 31; in each aligned block of 64 rows (0 to 63, 64 to 127, ...) at most 4 rows name the same one
- left_stats: float32 [128, 512, 512], P('dp', 'replica'), may hold values from -12 to 12
- right_stats: float32 [128, 512, 512], P('dp', 'replica'), may hold values from -12 to 12
- second_moment: float32 [128, 512, 512], P('dp', 'replica'), may hold values from 0.1 to 10
- left_root: bfloat16 [128, 512, 512], P('dp', 'replica'), may hold values from -1 to 4, as said below
- right_root: bfloat16 [128, 512, 512], P('dp', 'replica'), may hold values from -1 to 4, as said below
Outputs:
- left_new: float32 [128, 512, 512], P('dp', 'replica')
- right_new: float32 [128, 512, 512], P('dp', 'replica')
- moment_new: float32 [128, 512, 512], P('dp', 'replica')
- direction: bfloat16 [128, 512, 512], P('dp', 'replica')
The draws below stay inside these ranges and needn't reach their ends.
Inputs may be any that keep to these rules, and one draw needn't show every extreme that they name: `assignment`: no owner is named by more than 4 blocks, a bound that some block reaches. `left_root`: each slot's matrix is symmetric. `right_root`: each slot's matrix is symmetric.
All inputs are finite; a program needn't handle non-finite values.
Results may differ from the reference program's by a relative error of at most 0.025.
Values may be sent and summed in bfloat16 or wider, within the bound.
A program may use at most 32 MiB of HBM per device.

```python
import math
import jax
import jax.numpy as jnp
import numpy as np
from jax import lax

B = 512
MOST = 4
NB = 64
SLOTS = 128
N_DP = 32


def symmetric_root(key, lowest, highest, spread):
    first, second = jax.random.split(key)
    noise = jax.random.normal(first, (SLOTS, B, B), jnp.float32)
    mirror = (noise + jnp.swapaxes(noise, 1, 2)) * (spread / (2.0 * B) ** 0.5)
    mirror = jnp.clip(mirror, -1.0, 1.0)
    logs = jax.random.uniform(second, (SLOTS, B), jnp.float32, jnp.log(lowest), jnp.log(highest))
    eye = jnp.eye(B, dtype=jnp.float32)[None, :, :]
    matrix = mirror * (1.0 - eye) + eye * jnp.exp(logs)[:, :, None]
    return matrix.astype(jnp.bfloat16)


def draw_left_root(key, part):
    key = jax.random.fold_in(key, 11)
    return symmetric_root(key, 0.5, 2.0, 0.5)


def draw_right_root(key, part):
    key = jax.random.fold_in(key, 12)
    return symmetric_root(key, 0.5, 2.0, 0.5)


def block_levels(key, extent, cuts, low, largest):
    def one(dim, shards_of):
        steps = jax.random.uniform(jax.random.fold_in(jax.random.fold_in(key, 6), dim), (shards_of,), jnp.float32, low / len(cuts), largest / len(cuts))
        return jnp.repeat(jnp.exp(steps), extent[dim] // shards_of).reshape((-1,) + (1,) * (len(extent) - dim - 1))

    loudness = one(*cuts[0])
    for cut in cuts[1:]:
        loudness = loudness * one(*cut)
    return loudness


def shared_out(stream_key, own, number, rows, count, top, most, lean):
    order = jax.random.permutation(stream_key, count)
    crowded, ordinary = load_shares(count, rows * top, most, lean, True), load_shares(count, rows * top, most, lean, False)
    places = jnp.arange(count)

    def named(lengths, turn):
        used = int((lengths > 0).sum())
        fixed = max(1, used // 4)
        passed = fixed + (places - fixed + turn * (used - fixed)) % max(1, count - fixed)
        return jnp.zeros((count,), jnp.int32).at[order[jnp.where(places < fixed, places, passed)]].set(jnp.asarray(lengths, jnp.int32))

    lengths = jnp.where(number % 4 == 0, named(crowded, number // 4), named(ordinary, number - number // 4 - 1))
    mixed = jax.random.permutation(jax.random.fold_in(own, 3), count)
    source_of, receiver = mixed[0:count // 2 * 2:2], mixed[1:count // 2 * 2:2]
    room = jnp.minimum(lengths[source_of] - 1, most - lengths[receiver]) // 2
    room = jnp.where((source_of == order[0]) | (receiver == order[0]) | (lengths[receiver] == 0), 0, jnp.maximum(room, 0))
    passed = jax.random.randint(jax.random.fold_in(own, 4), (count // 2,), 0, 1 << 20) % (room + 1)
    lengths = lengths.at[source_of].add(-passed).at[receiver].add(passed)
    labels = jnp.searchsorted(jnp.cumsum(lengths), jnp.arange(rows * top), side="right").astype(jnp.int32)
    listing = labels.reshape(top, rows).T
    listing = listing[jax.random.permutation(jax.random.fold_in(own, 1), rows)]
    turn = jax.random.randint(jax.random.fold_in(own, 2), (rows, 1), 0, top)
    return jnp.take_along_axis(listing, (jnp.arange(top)[None, :] + turn) % top, axis=1)


def load_shares(number_of, total, bound, slope, full):
    portions = [(1 << 20) // math.isqrt(grade ** slope) + 1 for grade in range(1, number_of + 1)]
    largest = bound if full else min(bound, max(-(-total // number_of), total * portions[0] // sum(portions)))
    least = 1 if total - largest >= number_of - 1 else 0
    counts, spare = [largest] + [least] * (number_of - 1), total - largest - least * (number_of - 1)
    while spare > 0:
        movable = [i for i in range(1, number_of) if counts[i] < largest] or [i for i in range(1, number_of) if counts[i] < bound]
        whole, budget = sum([portions[i] for i in movable]), spare
        for i in movable:
            more = min(bound - counts[i], max(1, budget * portions[i] // whole), spare)
            counts[i] = counts[i] + more
            spare = spare - more
    return np.array(counts)


def gaussian(key, dims, deviation, most, cuts=(), kind=jnp.bfloat16):
    values = jax.random.normal(key, dims, jnp.float32) * deviation
    if len(cuts) > 0:
        values = block_levels(key, dims, cuts, -0.22, 0.18) * values
    return jnp.clip(values, min=-most, max=most).astype(kind)


def setup_inputs(seed: int = 0) -> dict:
    seeds = jax.random.split(jax.random.key(seed), 8)
    grads = gaussian(seeds[0], (N_DP, NB, B, B), 0.18, 2.5, ((0, 32), (2, 32)))
    assignment_keys = jax.random.split(jax.random.fold_in(seeds[1], 1), NB // NB)
    assignment_turns = jax.random.permutation(jax.random.fold_in(seeds[1], 3), NB // NB)
    assignment = jax.vmap(lambda own, number: shared_out(jax.random.fold_in(seeds[1], 2), own, number, NB, N_DP, 1, MOST, 2))(assignment_keys, assignment_turns).reshape((NB, 1))
    left_stats = gaussian(seeds[2], (SLOTS, B, B), 2.0, 12.0, ((0, 32), (1, 32)), jnp.float32)
    right_stats = gaussian(seeds[3], (SLOTS, B, B), 2.0, 12.0, ((0, 32), (1, 32)), jnp.float32)
    second_moment = jnp.clip(jnp.exp(math.log(10.0) - 4.6051702 * jax.random.uniform(seeds[4], (SLOTS, B, B), jnp.float32) ** block_levels(seeds[4], (SLOTS, B, B), ((0, 32), (1, 32)), -0.2, 0.2)), 0.1, 10.0)
    left_root = draw_left_root(jax.random.fold_in(seeds[7], 71), 0)
    right_root = draw_right_root(jax.random.fold_in(seeds[7], 71), 0)
    return dict(grads=grads, assignment=assignment, left_stats=left_stats, right_stats=right_stats, second_moment=second_moment, left_root=left_root, right_root=right_root)


def slot_of(assignment):
    owner = assignment[:, 0]
    onehot = (owner[:, None] == jnp.arange(N_DP, dtype=jnp.int32)[None, :]).astype(jnp.int32)
    before = jnp.cumsum(onehot, axis=0) - onehot
    rank = lax.optimization_barrier(jnp.sum(before * onehot, axis=1)).astype(jnp.int32)
    return (owner * MOST + rank).astype(jnp.int32)

def reference(grads, assignment, left_stats, right_stats, second_moment, left_root, right_root):

    def add_shard(index, total):
        return total + grads[index].astype(jnp.float32)
    total = lax.fori_loop(0, N_DP, add_shard, jnp.zeros((NB, B, B), jnp.float32))
    slot = slot_of(assignment)
    summed = jnp.zeros((SLOTS, B, B), jnp.float32).at[slot].set(total)
    low = summed.astype(jnp.bfloat16)

    def one_slot(items):
        grad, left, right, moment, lroot, rroot = items
        wide = grad.astype(jnp.float32)
        left_next = 0.9 * left + 0.1 * jnp.dot(grad, grad.T, preferred_element_type=jnp.float32)
        right_next = 0.9 * right + 0.1 * jnp.dot(grad.T, grad, preferred_element_type=jnp.float32)
        moment_next = 0.95 * moment + 0.05 * wide * wide
        adam = wide / (jnp.sqrt(moment_next) + 1e-08)
        left_product = jnp.dot(lroot, grad, preferred_element_type=jnp.float32).astype(jnp.bfloat16)
        shaped = jnp.dot(left_product, rroot, preferred_element_type=jnp.float32)
        ratio = jnp.sqrt(jnp.mean(adam * adam)) / jnp.sqrt(jnp.mean(shaped * shaped) + 1e-06)
        return (left_next, right_next, moment_next, (shaped * ratio).astype(jnp.bfloat16))
    left_new, right_new, moment_new, direction = lax.map(one_slot, (low, left_stats, right_stats, second_moment, left_root, right_root))
    return (left_new, right_new, moment_new, direction)
```

```python
import jax
import jax.numpy as jnp
from jax import lax
from jax.experimental import pallas as pl
from jax.experimental.pallas import tpu as pltpu
from jax.sharding import PartitionSpec as P

MESH = pl.DeviceIdType.MESH
NX, NY, NZ, NC = 4, 8, 16, 2
MOST, ROWS, WIDTH, BLOCKS = 4, 16, 512, 64
FAR = (4, 12, 8)
NEAR = (1, 15, 2)


def nt(a, b):
    return lax.dot_general(a, b, (((1,), (1,)), ((), ())), preferred_element_type=jnp.float32)


def nn(a, b):
    return lax.dot_general(a, b, (((1,), (0,)), ((), ())), preferred_element_type=jnp.float32)


def kernel(
    source, grads, left_stats, right_stats, moment, left_root, right_root,
    left_new, right_new, moment_new, direction,
    blocks, sendx, recvx, sendy, recvy, full, root, shaped, tally,
    load_sem, xs, xr, ys, yr, fs, fr, ns, nr, cs, cr, ts, tr,
):
    d, r = lax.axis_index("dp"), lax.axis_index("replica")
    x, y, z, c = d // NY, d % NY, r // NC, r % NC
    zhi, zlo = z // 4, z % 4

    def at(dx=0, dy=0, dz=0, dc=0):
        return (((x + dx) % NX) * NY + (y + dy) % NY, ((z + dz) % NZ) * NC + (c + dc) % NC)

    def copy(src, dst, s, e, target):
        return pltpu.make_async_remote_copy(
            src_ref=src, dst_ref=dst, send_sem=s, recv_sem=e, device_id=target, device_id_type=MESH
        )

    load = pltpu.make_async_copy(grads, blocks.at[pl.ds(0, BLOCKS)], load_sem.at[0])
    load.start()

    barrier = pltpu.get_barrier_semaphore()
    for i in range(1, NX):
        pl.semaphore_signal(barrier, inc=1, device_id=at(dx=i), device_id_type=MESH)
    for i in range(1, NY):
        pl.semaphore_signal(barrier, inc=1, device_id=at(dy=i), device_id_type=MESH)

    def greet(i, carry):
        pl.semaphore_signal(barrier, inc=1, device_id=at(dz=i // 2, dc=i % 2), device_id_type=MESH)
        return carry

    lax.fori_loop(1, NZ * NC, greet, 0)

    blocks[BLOCKS] = jnp.zeros((ROWS, WIDTH), jnp.bfloat16)
    root[:, zhi, zlo, c] = right_root[...]
    load.wait()

    def pick(k):
        def one(i, carry):
            to, row = i // NY, i % NY
            sendx[k, to, row] = blocks[source[(((x + to) % NX) * NY + row) * MOST + k]]
            return carry

        lax.fori_loop(0, NX * NY, one, 0)

    def x_copy(k, i):
        return copy(sendx.at[k, i], recvx.at[k, i - 1], xs.at[k, i - 1], xr.at[k, i - 1], at(dx=i))

    def x_send(k):
        for i in range(1, NX):
            x_copy(k, i).start()

    def x_sum(k):
        for i in range(1, NX):
            x_copy(k, i).wait_recv()

        def one(row, carry):
            total = sendx[k, 0, row].astype(jnp.float32)
            for i in range(NX - 1):
                total += recvx[k, i, row].astype(jnp.float32)
            sendy[k, row] = total.astype(jnp.bfloat16)
            return carry

        lax.fori_loop(0, NY, one, 0)

    def y_copy(k, i):
        return copy(
            sendy.at[k, (y + i) % NY], recvy.at[k, i - 1], ys.at[k, i - 1], yr.at[k, i - 1], at(dy=i)
        )

    def y_send(k):
        for i in range(1, NY):
            y_copy(k, i).start()

    def far_copy(ref, k, n, i):
        piece = ref.at[k, zhi, zlo, c]
        return copy(piece, piece, fs.at[n, i], fr.at[n, i], at(dz=FAR[i]))

    def near_copy(ref, k, n, i):
        piece = ref.at[k, :, zlo, c]
        return copy(piece, piece, ns.at[n, i], nr.at[n, i], at(dz=NEAR[i]))

    def twin_copy(ref, k, n, i):
        piece = ref.at[k, :, zlo, c] if i == 0 else ref.at[k, :, (z - NEAR[i - 1]) % 4, c]
        return copy(piece, piece, cs.at[n, i], cr.at[n, i], at(dc=1))

    def far(ref, k, n):
        for i in range(3):
            far_copy(ref, k, n, i).start()

    def near(ref, k, n):
        for i in range(3):
            far_copy(ref, k, n, i).wait_recv()
        for i in range(3):
            near_copy(ref, k, n, i).start()
        twin_copy(ref, k, n, 0).start()

    def twin(ref, k, n):
        for i in range(3):
            near_copy(ref, k, n, i).wait_recv()
            twin_copy(ref, k, n, i + 1).start()

    def gathered(ref, k, n):
        for i in range(4):
            twin_copy(ref, k, n, i).wait_recv()

    def y_sum(k):
        for i in range(1, NY):
            y_copy(k, i).wait_recv()
        total = sendy[k, y].astype(jnp.float32)
        for i in range(NY - 1):
            total += recvy[k, i].astype(jnp.float32)
        full[k, zhi, zlo, c] = total.astype(jnp.bfloat16)
        far(full, k, k)

    everything = pl.ds(0, MOST)
    lane = lax.broadcasted_iota(jnp.int32, (1, 128), 1)
    sums = jnp.zeros((1, 128), jnp.float32)

    pick(0)
    pl.semaphore_wait(barrier, NX - 1 + NY - 1 + NZ * NC - 1)
    x_send(0)
    far(root, everything, MOST)
    pick(1)
    x_send(1)
    pick(2)
    pick(3)
    x_sum(0)
    x_send(2)
    y_send(0)
    near(root, everything, MOST)
    x_sum(1)
    x_send(3)
    y_send(1)
    y_sum(0)
    x_sum(2)
    y_send(2)
    y_sum(1)
    near(full, 0, 0)
    twin(root, everything, MOST)
    x_sum(3)
    y_send(3)
    y_sum(2)
    near(full, 1, 1)
    y_sum(3)
    for k in range(MOST):
        wide = full[k, zhi, zlo, c].astype(jnp.float32)
        fresh = 0.95 * moment[k] + 0.05 * wide * wide
        moment_new[k] = fresh
        adam = wide / (jnp.sqrt(fresh) + 1e-08)
        sums += jnp.where(lane == k, jnp.sum(adam * adam), 0.0)
    twin(full, 0, 0)
    near(full, 2, 2)
    twin(full, 1, 1)
    near(full, 3, 3)

    base = z * (NC * ROWS) + c * ROWS
    chosen = lax.broadcasted_iota(jnp.int32, (ROWS, WIDTH), 1) == base + lax.broadcasted_iota(
        jnp.int32, (ROWS, WIDTH), 0
    )
    pick_cols = jnp.where(chosen, 1.0, 0.0).astype(jnp.bfloat16)

    gathered(root, everything, MOST)
    for k in range(MOST):
        if k >= 2:
            twin(full, k, k)
        gathered(full, k, k)
        block = full[k].reshape(WIDTH, WIDTH)
        across = nt(jnp.concatenate([full[k, zhi, zlo, c], pick_cols], axis=0), block)
        left_new[k] = 0.9 * left_stats[k] + 0.1 * across[:ROWS]
        own_cols = across[ROWS:].astype(jnp.bfloat16)
        down = nn(jnp.concatenate([left_root[k], own_cols], axis=0), block)
        right_new[k] = 0.9 * right_stats[k] + 0.1 * down[ROWS:]
        part = nn(down[:ROWS].astype(jnp.bfloat16), root[k].reshape(WIDTH, WIDTH))
        shaped[k] = part
        sums += jnp.where(lane == MOST + k, jnp.sum(part * part), 0.0)

    tally[0] = sums

    def tally_copy(i):
        return copy(
            tally.at[0], tally.at[i], ts.at[i - 1], tr.at[i - 1], at(dz=i // 2, dc=i % 2)
        )

    def tally_start(i, carry):
        tally_copy(i).start()
        return carry

    def tally_wait(i, carry):
        tally_copy(i).wait()
        return carry

    lax.fori_loop(1, NZ * NC, tally_start, 0)
    lax.fori_loop(1, NZ * NC, tally_wait, 0)
    totals = jnp.sum(tally[...], axis=0)
    entries = float(WIDTH * WIDTH)
    for k in range(MOST):
        adam_total = jnp.sum(jnp.where(lane == k, totals, 0.0), axis=1, keepdims=True)
        shaped_total = jnp.sum(jnp.where(lane == MOST + k, totals, 0.0), axis=1, keepdims=True)
        ratio = jnp.sqrt(adam_total / entries) / jnp.sqrt(shaped_total / entries + 1e-06)
        direction[k] = (shaped[k] * ratio).astype(jnp.bfloat16)

    for k in range(MOST):
        for i in range(1, NX):
            x_copy(k, i).wait_send()
        for i in range(1, NY):
            y_copy(k, i).wait_send()
    for ref, k, n in [(full, k, k) for k in range(MOST)] + [(root, everything, MOST)]:
        for i in range(3):
            far_copy(ref, k, n, i).wait_send()
            near_copy(ref, k, n, i).wait_send()
        for i in range(4):
            twin_copy(ref, k, n, i).wait_send()


def on_device(grads, assignment, left_stats, right_stats, second_moment, left_root, right_root):
    owner = assignment[:, 0]
    numbers = jnp.arange(BLOCKS, dtype=jnp.int32)
    same = (owner[:, None] == owner[None, :]) & (numbers[None, :] < numbers[:, None])
    slot = owner * MOST + jnp.sum(same.astype(jnp.int32), axis=1)
    slots = NX * NY * MOST
    match = (slot[:, None] == jnp.arange(slots, dtype=jnp.int32)[None, :]).astype(jnp.int32)
    source = BLOCKS + jnp.sum(match * (numbers[:, None] - BLOCKS), axis=0)

    vmem = pl.BlockSpec(memory_space=pltpu.VMEM)
    wide = jax.ShapeDtypeStruct((MOST, ROWS, WIDTH), jnp.float32)
    dma = pltpu.SemaphoreType.DMA
    gathers = MOST + 1
    return pl.pallas_call(
        kernel,
        name="shampoo",
        out_shape=[wide, wide, wide, jax.ShapeDtypeStruct((MOST, ROWS, WIDTH), jnp.bfloat16)],
        in_specs=[pl.BlockSpec(memory_space=pltpu.SMEM), pl.BlockSpec(memory_space=pl.ANY)] + [vmem] * 5,
        out_specs=[vmem] * 4,
        scratch_shapes=[
            pltpu.VMEM((BLOCKS + 1, ROWS, WIDTH), jnp.bfloat16),
            pltpu.VMEM((MOST, NX, NY, ROWS, WIDTH), jnp.bfloat16),
            pltpu.VMEM((MOST, NX - 1, NY, ROWS, WIDTH), jnp.bfloat16),
            pltpu.VMEM((MOST, NY, ROWS, WIDTH), jnp.bfloat16),
            pltpu.VMEM((MOST, NY - 1, ROWS, WIDTH), jnp.bfloat16),
            pltpu.VMEM((MOST, 4, 4, NC, ROWS, WIDTH), jnp.bfloat16),
            pltpu.VMEM((MOST, 4, 4, NC, ROWS, WIDTH), jnp.bfloat16),
            pltpu.VMEM((MOST, ROWS, WIDTH), jnp.float32),
            pltpu.VMEM((NZ * NC, 1, 128), jnp.float32),
            dma((1,)),
            dma((MOST, NX - 1)),
            dma((MOST, NX - 1)),
            dma((MOST, NY - 1)),
            dma((MOST, NY - 1)),
            dma((gathers, 3)),
            dma((gathers, 3)),
            dma((gathers, 3)),
            dma((gathers, 3)),
            dma((gathers, 4)),
            dma((gathers, 4)),
            dma((NZ * NC - 1,)),
            dma((NZ * NC - 1,)),
        ],
        compiler_params=pltpu.CompilerParams(
            collective_id=0, has_side_effects=True, vmem_limit_bytes=32 << 20
        ),
        cost_estimate=pl.CostEstimate(flops=140_000_000, bytes_accessed=2_400_000, transcendentals=70_000),
    )(source, grads[0], left_stats, right_stats, second_moment, left_root, right_root)


def solution(mesh):
    rows = P("dp", "replica", None)
    return jax.shard_map(
        on_device,
        mesh=mesh,
        in_specs=(P("dp", None, "replica", None), P(), rows, rows, rows, rows, rows),
        out_specs=(rows,) * 4,
        check_vma=False,
    )
```

```python
import jax
import jax.numpy as jnp
from jax import lax
from jax.experimental import pallas as pl
from jax.experimental.pallas import tpu as pltpu
from jax.sharding import PartitionSpec as P

MESH = pl.DeviceIdType.MESH
NX, NY, NZ, NC = 4, 8, 16, 2
MOST, ROWS, WIDTH, BLOCKS = 4, 16, 512, 64
XFIRST = 3
NEAR = (0, -1, 1, 2)


def nt(a, b):
    return lax.dot_general(a, b, (((1,), (1,)), ((), ())), preferred_element_type=jnp.float32)


def nn(a, b):
    return lax.dot_general(a, b, (((1,), (0,)), ((), ())), preferred_element_type=jnp.float32)


def kernel(
    source, grads, left_stats, right_stats, moment, left_root, right_root,
    left_new, right_new, moment_new, direction,
    blocks, stats, mine, sendx, recvx, sendy, recvy, sendq, recvq, sendr, recvr,
    low, full, roots, outbox, inbox, norms, tally,
    load_sem, xs, xr, ys, yr, qs, qr, ps, pr, rs, rr, us, ur, gs, gr, cs, cr, ns, nr, ms, mr, ts, tr,
):
    d, r = lax.axis_index("dp"), lax.axis_index("replica")
    x, y, z, c = d // NY, d % NY, r // NC, r % NC

    def at(dx=0, dy=0, dz=0, dc=0):
        return (((x + dx) % NX) * NY + (y + dy) % NY, ((z + dz) % NZ) * NC + (c + dc) % NC)

    def copy(src, dst, s, e, target):
        return pltpu.make_async_remote_copy(
            src_ref=src, dst_ref=dst, send_sem=s, recv_sem=e, device_id=target, device_id_type=MESH
        )

    def loop(start, stop, body):
        def step(i, carry):
            body(i)
            return carry

        lax.fori_loop(start, stop, step, 0)

    loads = [
        pltpu.make_async_copy(a, b, load_sem.at[i])
        for i, (a, b) in enumerate((
            (grads, blocks.at[pl.ds(0, BLOCKS)]),
            (left_root, mine.at[:, 0]),
            (right_root, mine.at[:, 1]),
            (moment, stats.at[2]),
            (left_stats, stats.at[0]),
            (right_stats, stats.at[1]),
        ))
    ]
    for load in loads:
        load.start()

    barrier = pltpu.get_barrier_semaphore()
    for i in range(1, NX):
        pl.semaphore_signal(barrier, inc=1, device_id=at(dx=i), device_id_type=MESH)
    for i in range(1, NY):
        pl.semaphore_signal(barrier, inc=1, device_id=at(dy=i), device_id_type=MESH)
    loop(1, NZ * NC, lambda i: pl.semaphore_signal(
        barrier, inc=1, device_id=at(dz=i // 2, dc=i % 2), device_id_type=MESH
    ))

    blocks[BLOCKS] = jnp.zeros((ROWS, WIDTH), jnp.bfloat16)


    def pick(k):
        def one(i):
            to, row = i // NY, i % NY
            sendx[k, to, row] = blocks[source[(((x + to) % NX) * NY + row) * MOST + k]]

        loop(0, NX * NY, one)

    def x_copy(k, i):
        return copy(sendx.at[k, i], recvx.at[k, i - 1], xs.at[k, i - 1], xr.at[k, i - 1], at(dx=i))

    def x_send(k):
        for i in range(1, NX):
            x_copy(k, i).start()

    def x_sum(k):
        for i in range(1, NX):
            x_copy(k, i).wait_recv()

        def one(row):
            total = sendx[k, 0, row].astype(jnp.float32)
            for i in range(NX - 1):
                total += recvx[k, i, row].astype(jnp.float32)
            sendy[k, row] = total.astype(jnp.bfloat16)

        loop(0, NY, one)

    def y_copy(k, i):
        return copy(
            sendy.at[k, (y + i) % NY], recvy.at[k, i - 1], ys.at[k, i - 1], yr.at[k, i - 1], at(dy=i)
        )

    def y_send(k):
        for i in range(1, NY):
            y_copy(k, i).start()

    def y_sum(k):
        for i in range(1, NY):
            y_copy(k, i).wait_recv()
        total = sendy[k, y].astype(jnp.float32)
        for i in range(NY - 1):
            total += recvy[k, i].astype(jnp.float32)
        low[k] = total.astype(jnp.bfloat16)


    def pick_last():
        def one(i):
            to, row = i // NX, i % NX
            sendq[to, row] = blocks[source[(row * NY + (y + to) % NY) * MOST + XFIRST]]

        loop(0, NX * NY, one)

    def q_copy(i):
        return copy(sendq.at[i], recvq.at[i - 1], qs.at[i - 1], qr.at[i - 1], at(dy=i))

    def q_sum():
        for i in range(1, NY):
            q_copy(i).wait_recv()

        def one(row):
            total = sendq[0, row].astype(jnp.float32)
            for i in range(NY - 1):
                total += recvq[i, row].astype(jnp.float32)
            sendr[row] = total.astype(jnp.bfloat16)

        loop(0, NX, one)

    def p_copy(i):
        return copy(sendr.at[(x + i) % NX], recvr.at[i - 1], ps.at[i - 1], pr.at[i - 1], at(dx=i))

    def p_sum():
        for i in range(1, NX):
            p_copy(i).wait_recv()
        total = sendr[x].astype(jnp.float32)
        for i in range(NX - 1):
            total += recvr[i].astype(jnp.float32)
        low[XFIRST] = total.astype(jnp.bfloat16)


    def root_copy(dz):
        return copy(mine.at[(z + dz) % MOST], roots.at[:, z, c], rs.at[dz], rr.at[dz], at(dz=dz))

    def root_relay():
        lane = roots.at[:, :, c]
        return copy(lane, lane, us.at[0], ur.at[0], at(dc=1))

    def g_copy(k, dz):
        return copy(low.at[k], full.at[z, c], gs.at[dz], gr.at[dz], at(dz=dz))

    def g_send(k):
        first = (k - z) % MOST
        for j in range(1, NZ // MOST):
            g_copy(k, first + j * MOST).start()

        @pl.when(first != 0)
        def _():
            g_copy(k, first).start()

        @pl.when(first == 0)
        def _():
            full[z, c] = low[k]

    def g_relay(dz):
        piece = full.at[(z - dz) % NZ, c]
        return copy(piece, piece, cs.at[dz], cr.at[dz], at(dc=1))

    def g_pass(dz):
        g_copy(0, dz).wait_recv()
        g_relay(dz).start()

    def tally_copy(i):
        return copy(tally.at[0], tally.at[i], ts.at[i - 1], tr.at[i - 1], at(dz=i // 2, dc=i % 2))

    def near_copy(i):
        return copy(outbox.at[i], inbox.at[i], ns.at[i - 1], nr.at[i - 1], at(dz=NEAR[i]))

    def norm_copy(i):
        return copy(norms.at[0], norms.at[i], ms.at[i - 1], mr.at[i - 1], at(dz=NEAR[i]))

    loads[0].wait()
    pick(0)
    pick_last()
    pl.semaphore_wait(barrier, NX - 1 + NY - 1 + NZ * NC - 1)
    x_send(0)
    for i in range(1, NY):
        q_copy(i).start()
    loads[1].wait()
    loads[2].wait()
    loop(1, NZ, lambda dz: root_copy(dz).start())
    pick(1)
    x_send(1)
    roots[:, z, c] = mine[z % MOST]
    pick(2)
    x_sum(0)
    x_send(2)
    y_send(0)
    x_sum(1)
    y_send(1)
    q_sum()
    for i in range(1, NX):
        p_copy(i).start()
    y_sum(0)
    g_send(0)
    x_sum(2)
    y_send(2)
    p_sum()
    g_send(3)
    y_sum(1)
    g_send(1)
    y_sum(2)
    g_send(2)

    lane = lax.broadcasted_iota(jnp.int32, (1, 128), 1)
    sums = jnp.zeros((1, 128), jnp.float32)
    for load in loads[3:]:
        load.wait()
    for k in range(MOST):
        wide = low[k].astype(jnp.float32)
        fresh = 0.95 * stats[2, k] + 0.05 * wide * wide
        moment_new[k] = fresh
        adam = wide / (jnp.sqrt(fresh) + 1e-08)
        sums += jnp.where(lane == k, jnp.sum(adam * adam), 0.0)
    tally[0] = sums
    loop(1, NZ * NC, lambda i: tally_copy(i).start())

    loop(1, NZ, lambda dz: root_copy(dz).wait_recv())
    root_relay().start()
    g_relay(0).start()
    loop(1, NZ, g_pass)

    chosen = []
    for i in NEAR:
        base = ((z + i) % NZ) * (NC * ROWS) + c * ROWS
        rows = lax.broadcasted_iota(jnp.int32, (ROWS, WIDTH), 0) + base
        hit = lax.broadcasted_iota(jnp.int32, (ROWS, WIDTH), 1) == rows
        chosen.append(jnp.where(hit, 1.0, 0.0).astype(jnp.bfloat16))

    root_relay().wait_recv()
    loop(0, NZ, lambda dz: g_relay(dz).wait_recv())

    many = len(NEAR) * ROWS
    block = full[...].reshape(WIDTH, WIDTH)
    right = roots[1].reshape(WIDTH, WIDTH)
    across = nt(jnp.concatenate([full[(z + i) % NZ, c] for i in NEAR] + chosen, axis=0), block)
    cols = across[many:].astype(jnp.bfloat16)
    down = nn(
        jnp.concatenate([roots[0, (z + i) % NZ, c] for i in NEAR] + [cols], axis=0), block
    )
    part = nn(down[:many].astype(jnp.bfloat16), right)
    for i in range(len(NEAR)):
        at_i = slice(i * ROWS, (i + 1) * ROWS)
        box = inbox if i == 0 else outbox
        box[i, 0] = across[at_i].astype(jnp.bfloat16)
        box[i, 1] = down[many + i * ROWS:many + (i + 1) * ROWS].astype(jnp.bfloat16)
        box[i, 2] = part[at_i].astype(jnp.bfloat16)
        if i > 0:
            near_copy(i).start()

    squares = jnp.zeros((1, 1), jnp.float32)
    for i in range(2):
        half = roots[0, i * 8:(i + 1) * 8].reshape(WIDTH // 2, WIDTH)
        shaped = nn(nn(half, block).astype(jnp.bfloat16), right)
        squares += jnp.sum(shaped * shaped).reshape(1, 1)
    norms[0] = jnp.broadcast_to(squares, (1, 128))
    for i in range(1, len(NEAR)):
        norm_copy(i).start()

    for i in range(len(NEAR)):
        if i > 0:
            near_copy(i).wait_recv()
        k = (z - NEAR[i]) % MOST
        left_new[k] = 0.9 * stats[0, k] + 0.1 * inbox[i, 0].astype(jnp.float32)
        right_new[k] = 0.9 * stats[1, k] + 0.1 * inbox[i, 1].astype(jnp.float32)

    loop(1, NZ * NC, lambda i: tally_copy(i).wait())
    totals = jnp.sum(tally[...], axis=0)
    entries = float(WIDTH * WIDTH)
    for i in range(len(NEAR)):
        if i > 0:
            norm_copy(i).wait_recv()
        k = (z - NEAR[i]) % MOST
        adam_total = jnp.sum(jnp.where(lane == k, totals, 0.0), axis=1, keepdims=True)
        ratio = jnp.sqrt(adam_total / entries) / jnp.sqrt(norms[i][:, :1] / entries + 1e-06)
        direction[k] = (inbox[i, 2].astype(jnp.float32) * ratio).astype(jnp.bfloat16)

    for k in range(XFIRST):
        for i in range(1, NX):
            x_copy(k, i).wait_send()
        for i in range(1, NY):
            y_copy(k, i).wait_send()
    for i in range(1, NY):
        q_copy(i).wait_send()
    for i in range(1, NX):
        p_copy(i).wait_send()
    root_relay().wait_send()
    g_relay(0).wait_send()

    def sent(dz):
        root_copy(dz).wait_send()
        g_copy(0, dz).wait_send()
        g_relay(dz).wait_send()

    loop(1, NZ, sent)
    for i in range(1, len(NEAR)):
        near_copy(i).wait_send()
        norm_copy(i).wait_send()


def on_device(grads, assignment, left_stats, right_stats, second_moment, left_root, right_root):
    owner = assignment[:, 0]
    numbers = jnp.arange(BLOCKS, dtype=jnp.int32)
    same = (owner[:, None] == owner[None, :]) & (numbers[None, :] < numbers[:, None])
    slot = owner * MOST + jnp.sum(same.astype(jnp.int32), axis=1)
    slots = NX * NY * MOST
    match = (slot[:, None] == jnp.arange(slots, dtype=jnp.int32)[None, :]).astype(jnp.int32)
    source = BLOCKS + jnp.sum(match * (numbers[:, None] - BLOCKS), axis=0)

    wide = jax.ShapeDtypeStruct((MOST, ROWS, WIDTH), jnp.float32)
    narrow = jnp.bfloat16
    dma = pltpu.SemaphoreType.DMA
    tile = (ROWS, WIDTH)
    near = len(NEAR)

    def pair(*shape):
        return [dma(shape), dma(shape)]

    return pl.pallas_call(
        kernel,
        name="shampoo",
        out_shape=[wide, wide, wide, jax.ShapeDtypeStruct((MOST, ROWS, WIDTH), narrow)],
        in_specs=[pl.BlockSpec(memory_space=pltpu.SMEM)] + [pl.BlockSpec(memory_space=pl.ANY)] * 6,
        out_specs=[pl.BlockSpec(memory_space=pltpu.VMEM)] * 4,
        scratch_shapes=[
            pltpu.VMEM((BLOCKS + 1, *tile), narrow),
            pltpu.VMEM((3, MOST, *tile), jnp.float32),
            pltpu.VMEM((MOST, 2, *tile), narrow),
            pltpu.VMEM((XFIRST, NX, NY, *tile), narrow),
            pltpu.VMEM((XFIRST, NX - 1, NY, *tile), narrow),
            pltpu.VMEM((XFIRST, NY, *tile), narrow),
            pltpu.VMEM((XFIRST, NY - 1, *tile), narrow),
            pltpu.VMEM((NY, NX, *tile), narrow),
            pltpu.VMEM((NY - 1, NX, *tile), narrow),
            pltpu.VMEM((NX, *tile), narrow),
            pltpu.VMEM((NX - 1, *tile), narrow),
            pltpu.VMEM((MOST, *tile), narrow),
            pltpu.VMEM((NZ, NC, *tile), narrow),
            pltpu.VMEM((2, NZ, NC, *tile), narrow),
            pltpu.VMEM((near, 3, *tile), narrow),
            pltpu.VMEM((near, 3, *tile), narrow),
            pltpu.VMEM((near, 1, 128), jnp.float32),
            pltpu.VMEM((NZ * NC, 1, 128), jnp.float32),
            dma((6,)),
            *pair(XFIRST, NX - 1),
            *pair(XFIRST, NY - 1),
            *pair(NY - 1),
            *pair(NX - 1),
            *pair(NZ),
            *pair(1),
            *pair(NZ),
            *pair(NZ),
            *pair(near - 1),
            *pair(near - 1),
            *pair(NZ * NC - 1),
        ],
        compiler_params=pltpu.CompilerParams(
            collective_id=0, has_side_effects=True, vmem_limit_bytes=56 << 20
        ),
        cost_estimate=pl.CostEstimate(flops=800_000_000, bytes_accessed=2_400_000, transcendentals=70_000),
    )(source, grads[0], left_stats, right_stats, second_moment, left_root, right_root)


def solution(mesh):
    rows = P("dp", "replica", None)
    return jax.shard_map(
        on_device,
        mesh=mesh,
        in_specs=(P("dp", None, "replica", None), P(), rows, rows, rows, rows, rows),
        out_specs=(rows,) * 4,
        check_vma=False,
    )
```

```python
import functools

import jax
import jax.numpy as jnp
from jax import lax
from jax.experimental import pallas as pl
from jax.experimental.pallas import tpu as pltpu
from jax.sharding import PartitionSpec as P

MESH = pl.DeviceIdType.MESH
NX, NY, NZ, NC = 4, 8, 16, 2
MOST, ROWS, WIDTH, BLOCKS = 4, 16, 512, 64
XFIRST = 2
REST = MOST - XFIRST
CROWD = REST * NX
NEAR = (0, -1, 1, 2)


def nt(a, b):
    return lax.dot_general(a, b, (((1,), (1,)), ((), ())), preferred_element_type=jnp.float32)


def nn(a, b):
    return lax.dot_general(a, b, (((1,), (0,)), ((), ())), preferred_element_type=jnp.float32)


def kernel(
    cap, table, grads, left_stats, right_stats, moment, left_root, right_root,
    left_new, right_new, moment_new, direction,
    fresh, turned, blocks, stats, mine, sendx, recvx, sendy, recvy, sendq, recvq, crowd, sendr, recvr,
    low, full, roots, lefts, outbox, inbox, pair, tally,
    load_sem, save_sem, xs, xr, ys, yr, qs, qr, ps, pr, rs, rr, us, ur, gs, gr, cs, cr, ns, nr, ls, lr, vs, vr, ts, tr,
):
    d, r = lax.axis_index("dp"), lax.axis_index("replica")
    x, y, z, c = d // NY, d % NY, r // NC, r % NC

    def at(dx=0, dy=0, dz=0, dc=0):
        return (((x + dx) % NX) * NY + (y + dy) % NY, ((z + dz) % NZ) * NC + (c + dc) % NC)

    def copy(src, dst, s, e, target):
        return pltpu.make_async_remote_copy(
            src_ref=src, dst_ref=dst, send_sem=s, recv_sem=e, device_id=target, device_id_type=MESH
        )

    def loop(start, stop, body):
        def step(i, carry):
            body(i)
            return carry

        lax.fori_loop(start, stop, step, 0)

    loads = [
        pltpu.make_async_copy(a, b, load_sem.at[i])
        for i, (a, b) in enumerate((
            (grads, blocks.at[pl.ds(0, BLOCKS)]),
            (left_root, mine.at[0]),
            (right_root, mine.at[1]),
            (moment, stats.at[2]),
            (left_stats, stats.at[0]),
            (right_stats, stats.at[1]),
        ))
    ]
    for load in loads:
        load.start()

    saves = [
        pltpu.make_async_copy(a, b, save_sem.at[i])
        for i, (a, b) in enumerate((
            (fresh.at[0], left_new),
            (fresh.at[1], right_new),
            (fresh.at[2], moment_new),
            (turned, direction),
        ))
    ]

    barrier = pltpu.get_barrier_semaphore()
    for i in range(1, NX):
        pl.semaphore_signal(barrier, inc=1, device_id=at(dx=i), device_id_type=MESH)
    for i in range(1, NY):
        pl.semaphore_signal(barrier, inc=1, device_id=at(dy=i), device_id_type=MESH)
    loop(1, NZ, lambda i: pl.semaphore_signal(
        barrier, inc=1, device_id=at(dz=i), device_id_type=MESH
    ))
    pl.semaphore_signal(barrier, inc=1, device_id=at(dc=1), device_id_type=MESH)

    blocks[BLOCKS] = jnp.zeros((ROWS, WIDTH), jnp.bfloat16)
    crowd[CROWD] = jnp.zeros((ROWS, WIDTH), jnp.bfloat16)


    def pick(k):
        def one(i):
            to, row = i // NY, i % NY
            sendx[k, to, row] = blocks[table[(((x + to) % NX) * NY + row) * XFIRST + k]]

        loop(0, NX * NY, one)

    def x_copy(k, i):
        return copy(sendx.at[k, i], recvx.at[k, i - 1], xs.at[k, i - 1], xr.at[k, i - 1], at(dx=i))

    def x_send(k):
        for i in range(1, NX):
            x_copy(k, i).start()

    def x_sum(k):
        for i in range(1, NX):
            x_copy(k, i).wait_recv()

        def one(row):
            total = sendx[k, 0, row].astype(jnp.float32)
            for i in range(NX - 1):
                total += recvx[k, i, row].astype(jnp.float32)
            sendy[k, row] = total.astype(jnp.bfloat16)

        loop(0, NY, one)

    def y_copy(k, i):
        return copy(
            sendy.at[k, (y + i) % NY], recvy.at[k, i - 1], ys.at[k, i - 1], yr.at[k, i - 1], at(dy=i)
        )

    def y_send(k):
        for i in range(1, NY):
            y_copy(k, i).start()

    def y_sum(k):
        for i in range(1, NY):
            y_copy(k, i).wait_recv()
        total = sendy[k, y].astype(jnp.float32)
        for i in range(NY - 1):
            total += recvy[k, i].astype(jnp.float32)
        low[k] = total.astype(jnp.bfloat16)


    def pick_last():
        def one(i):
            to, row = i // cap, i % cap
            sendq[to, row] = blocks[table[BLOCKS + ((y + to) % NY) * CROWD + row]]

        loop(0, NY * cap, one)

    def q_copy(i):
        return copy(sendq.at[i], recvq.at[i - 1], qs.at[i - 1], qr.at[i - 1], at(dy=i))

    def q_sum():
        for i in range(1, NY):
            q_copy(i).wait_recv()

        def one(row):
            total = sendq[0, row].astype(jnp.float32)
            for i in range(NY - 1):
                total += recvq[i, row].astype(jnp.float32)
            crowd[row] = total.astype(jnp.bfloat16)

        loop(0, cap, one)

        def spread(i):
            to, row = i // REST, i % REST
            sendr[to, row] = crowd[table[2 * BLOCKS + (to * NY + y) * REST + row]]

        loop(0, NX * REST, spread)

    def p_copy(i):
        return copy(sendr.at[(x + i) % NX], recvr.at[i - 1], ps.at[i - 1], pr.at[i - 1], at(dx=i))

    def p_sum():
        for i in range(1, NX):
            p_copy(i).wait_recv()
        total = sendr[x].astype(jnp.float32)
        for i in range(NX - 1):
            total += recvr[i].astype(jnp.float32)
        low[pl.ds(XFIRST, REST)] = total.astype(jnp.bfloat16)


    def root_copy(dz):
        return copy(mine.at[1, (z + dz) % MOST], roots.at[z, c], rs.at[dz], rr.at[dz], at(dz=dz))

    def root_relay():
        lane = roots.at[:, c]
        return copy(lane, lane, us.at[0], ur.at[0], at(dc=1))

    def g_copy(k, dz):
        return copy(low.at[k], full.at[z, c], gs.at[dz], gr.at[dz], at(dz=dz))

    def g_send(k):
        first = (k - z) % MOST
        for j in range(1, NZ // MOST):
            g_copy(k, first + j * MOST).start()

        @pl.when(first != 0)
        def _():
            g_copy(k, first).start()

        @pl.when(first == 0)
        def _():
            full[z, c] = low[k]

    def g_relay():
        lane = full.at[:, c]
        return copy(lane, lane, cs.at[0], cr.at[0], at(dc=1))

    def tally_copy(i):
        return copy(tally.at[0], tally.at[i], ts.at[i], tr.at[i], at(dz=i))

    def pair_copy():
        return copy(pair.at[0], pair.at[1], ts.at[0], tr.at[0], at(dc=1))

    def near_copy(i):
        return copy(outbox.at[i], inbox.at[i], ns.at[i - 1], nr.at[i - 1], at(dz=NEAR[i]))

    def left_copy(i):
        return copy(
            mine.at[0, (z - NEAR[i]) % MOST], lefts.at[i, c], ls.at[i - 1], lr.at[i - 1], at(dz=-NEAR[i])
        )

    def left_relay():
        piece = lefts.at[:, c]
        return copy(piece, piece, vs.at[0], vr.at[0], at(dc=1))

    loads[0].wait()
    pick(0)
    pick_last()
    pl.semaphore_wait(barrier, NX - 1 + NY - 1 + NZ - 1 + NC - 1)
    x_send(0)
    for i in range(1, NY):
        q_copy(i).start()
    pick(1)
    x_send(1)
    loads[1].wait()
    loads[2].wait()
    loop(1, NZ, lambda dz: root_copy(dz).start())
    roots[z, c] = mine[1, z % MOST]
    lefts[0, c] = mine[0, z % MOST]
    for i in range(1, len(NEAR)):
        left_copy(i).start()
    x_sum(0)
    y_send(0)
    x_sum(1)
    y_send(1)
    y_sum(0)
    g_send(0)
    q_sum()
    for i in range(1, NX):
        p_copy(i).start()
    for i in range(1, len(NEAR)):
        left_copy(i).wait()
    left_relay().start()
    y_sum(1)
    g_send(1)
    p_sum()
    g_send(2)
    g_send(3)
    loop(1, NZ, lambda dz: root_copy(dz).wait_recv())
    root_relay().start()

    lane = lax.broadcasted_iota(jnp.int32, (1, 128), 1)
    sums = jnp.zeros((1, 128), jnp.float32)
    for load in loads[3:]:
        load.wait()
    for k in range(MOST):
        wide = low[k].astype(jnp.float32)
        second = 0.95 * stats[2, k] + 0.05 * wide * wide
        fresh[2, k] = second
        adam = wide / (jnp.sqrt(second) + 1e-08)
        sums += jnp.where(lane == k, jnp.sum(adam * adam), 0.0)
    saves[2].start()
    pair[0] = sums
    pair_copy().start()
    for k in range(XFIRST):
        for i in range(1, NX):
            x_copy(k, i).wait_send()
        for i in range(1, NY):
            y_copy(k, i).wait_send()
    for i in range(1, NY):
        q_copy(i).wait_send()
    for i in range(1, NX):
        p_copy(i).wait_send()
    loop(1, NZ, lambda dz: root_copy(dz).wait_send())

    loop(1, NZ, lambda dz: g_copy(0, dz).wait_recv())
    g_relay().start()

    chosen = []
    for i in NEAR:
        base = ((z + i) % NZ) * (NC * ROWS) + c * ROWS
        rows = lax.broadcasted_iota(jnp.int32, (ROWS, WIDTH), 0) + base
        hit = lax.broadcasted_iota(jnp.int32, (ROWS, WIDTH), 1) == rows
        chosen.append(jnp.where(hit, 1.0, 0.0).astype(jnp.bfloat16))

    root_relay().wait()
    left_relay().wait()
    pair_copy().wait()
    g_relay().wait()

    many = len(NEAR) * ROWS
    block = full[...].reshape(WIDTH, WIDTH)
    right = roots[...].reshape(WIDTH, WIDTH)
    across = nt(jnp.concatenate([full[(z + i) % NZ, c] for i in NEAR] + chosen, axis=0), block)
    cols = across[many:].astype(jnp.bfloat16)
    down = nn(
        jnp.concatenate(
            [lefts[i, c] for i in range(len(NEAR))] + [lefts[i, 1 - c] for i in range(len(NEAR))] + [cols], axis=0
        ),
        block,
    )
    part = nn(down[:2 * many].astype(jnp.bfloat16), right)
    tally[0] = pair[0] + pair[1] + jnp.where(lane == MOST + z % MOST, jnp.sum(part * part), 0.0)
    loop(1, NZ, lambda i: tally_copy(i).start())
    for i in range(len(NEAR)):
        at_i = slice(i * ROWS, (i + 1) * ROWS)
        box = inbox if i == 0 else outbox
        box[i, 0] = across[at_i].astype(jnp.bfloat16)
        box[i, 1] = down[2 * many + i * ROWS:2 * many + (i + 1) * ROWS].astype(jnp.bfloat16)
        box[i, 2] = part[at_i].astype(jnp.bfloat16)
        if i > 0:
            near_copy(i).start()

    for i in range(len(NEAR)):
        if i > 0:
            near_copy(i).wait_recv()
        k = (z - NEAR[i]) % MOST
        fresh[0, k] = 0.9 * stats[0, k] + 0.1 * inbox[i, 0].astype(jnp.float32)
        fresh[1, k] = 0.9 * stats[1, k] + 0.1 * inbox[i, 1].astype(jnp.float32)

    saves[0].start()
    saves[1].start()
    loop(1, NZ, lambda i: tally_copy(i).wait())
    totals = jnp.sum(tally[...], axis=0)
    entries = float(WIDTH * WIDTH)
    for i in range(len(NEAR)):
        k = (z - NEAR[i]) % MOST
        adam_total = jnp.sum(jnp.where(lane == k, totals, 0.0), axis=1, keepdims=True)
        shaped_total = jnp.sum(jnp.where(lane == MOST + k, totals, 0.0), axis=1, keepdims=True)
        ratio = jnp.sqrt(adam_total / entries) / jnp.sqrt(shaped_total / entries + 1e-06)
        turned[k] = (inbox[i, 2].astype(jnp.float32) * ratio).astype(jnp.bfloat16)
    saves[3].start()

    loop(1, NZ, lambda dz: g_copy(0, dz).wait_send())
    for i in range(1, len(NEAR)):
        near_copy(i).wait_send()
    for save in saves:
        save.wait()


def write(*refs):
    sems = refs[-1]
    half = len(refs) // 2
    copies = [pltpu.make_async_copy(refs[i], refs[half + i], sems.at[i]) for i in range(half)]
    for one in copies:
        one.start()
    for one in copies:
        one.wait()


def on_device(grads, assignment, left_stats, right_stats, second_moment, left_root, right_root):
    owner = assignment[:, 0]
    numbers = jnp.arange(BLOCKS, dtype=jnp.int32)
    earlier = numbers[None, :] < numbers[:, None]
    same = (owner[:, None] == owner[None, :]) & earlier
    rank = jnp.sum(same.astype(jnp.int32), axis=1)
    late = rank >= XFIRST
    beside = (owner[:, None] % NY == owner[None, :] % NY) & late[None, :] & earlier
    place = jnp.sum(beside.astype(jnp.int32), axis=1)

    def lookup(key, value, size, empty):
        match = key[:, None] == jnp.arange(size, dtype=jnp.int32)[None, :]
        return empty + jnp.sum(jnp.where(match, value[:, None] - empty, 0), axis=0)

    owners = NX * NY
    table = jnp.concatenate([
        lookup(jnp.where(late, -1, owner * XFIRST + rank), numbers, owners * XFIRST, BLOCKS),
        lookup(jnp.where(late, owner % NY * CROWD + place, -1), numbers, NY * CROWD, BLOCKS),
        lookup(jnp.where(late, owner * REST + rank - XFIRST, -1), place, owners * REST, CROWD),
    ])
    lean = CROWD // 2
    fits = jnp.max(jnp.where(late, place, 0)) < lean
    operands = (table, grads[0], left_stats, right_stats, second_moment, left_root, right_root)
    return lax.cond(
        fits,
        lambda *given: step(lean, 0, *given),
        lambda *given: step(CROWD, 1, *given),
        *operands,
    )


def step(cap, number, *operands):
    wide = jax.ShapeDtypeStruct((MOST, ROWS, WIDTH), jnp.float32)
    narrow = jnp.bfloat16
    dma = pltpu.SemaphoreType.DMA
    tile = (ROWS, WIDTH)
    near = len(NEAR)

    def pair(*shape):
        return [dma(shape), dma(shape)]

    outs = [wide, wide, wide, jax.ShapeDtypeStruct((MOST, ROWS, WIDTH), narrow)]
    results = pl.pallas_call(
        functools.partial(kernel, cap),
        name="shampoo",
        out_shape=outs,
        in_specs=[pl.BlockSpec(memory_space=pltpu.SMEM)] + [pl.BlockSpec(memory_space=pl.ANY)] * 6,
        out_specs=[pl.BlockSpec(memory_space=pl.ANY)] * 4,
        scratch_shapes=[
            pltpu.VMEM((3, MOST, *tile), jnp.float32),
            pltpu.VMEM((MOST, *tile), narrow),
            pltpu.VMEM((BLOCKS + 1, *tile), narrow),
            pltpu.VMEM((3, MOST, *tile), jnp.float32),
            pltpu.VMEM((2, MOST, *tile), narrow),
            pltpu.VMEM((XFIRST, NX, NY, *tile), narrow),
            pltpu.VMEM((XFIRST, NX - 1, NY, *tile), narrow),
            pltpu.VMEM((XFIRST, NY, *tile), narrow),
            pltpu.VMEM((XFIRST, NY - 1, *tile), narrow),
            pltpu.VMEM((NY, cap, *tile), narrow),
            pltpu.VMEM((NY - 1, cap, *tile), narrow),
            pltpu.VMEM((CROWD + 1, *tile), narrow),
            pltpu.VMEM((NX, REST, *tile), narrow),
            pltpu.VMEM((NX - 1, REST, *tile), narrow),
            pltpu.VMEM((MOST, *tile), narrow),
            pltpu.VMEM((NZ, NC, *tile), narrow),
            pltpu.VMEM((NZ, NC, *tile), narrow),
            pltpu.VMEM((near, NC, *tile), narrow),
            pltpu.VMEM((near, 3, *tile), narrow),
            pltpu.VMEM((near, 3, *tile), narrow),
            pltpu.VMEM((NC, 1, 128), jnp.float32),
            pltpu.VMEM((NZ, 1, 128), jnp.float32),
            dma((6,)),
            dma((4,)),
            *pair(XFIRST, NX - 1),
            *pair(XFIRST, NY - 1),
            *pair(NY - 1),
            *pair(NX - 1),
            *pair(NZ),
            *pair(1),
            *pair(NZ),
            *pair(1),
            *pair(near - 1),
            *pair(near - 1),
            *pair(1),
            *pair(NZ),
        ],
        compiler_params=pltpu.CompilerParams(
            collective_id=number, has_side_effects=True, vmem_limit_bytes=56 << 20
        ),
        cost_estimate=pl.CostEstimate(flops=800_000_000, bytes_accessed=2_400_000, transcendentals=70_000),
    )(*operands)
    return pl.pallas_call(
        write,
        name="write",
        out_shape=outs,
        in_specs=[pl.BlockSpec(memory_space=pltpu.VMEM)] * 4,
        out_specs=[pl.BlockSpec(memory_space=pl.ANY)] * 4,
        scratch_shapes=[dma((4,))],
    )(*results)


def solution(mesh):
    rows = P("dp", "replica", None)
    return jax.shard_map(
        on_device,
        mesh=mesh,
        in_specs=(P("dp", None, "replica", None), P(), rows, rows, rows, rows, rows),
        out_specs=(rows,) * 4,
        check_vma=False,
    )
```

```python
import functools

import jax
import jax.numpy as jnp
from jax import lax
from jax.experimental import pallas as pl
from jax.experimental.pallas import tpu as pltpu
from jax.sharding import PartitionSpec as P

MESH = pl.DeviceIdType.MESH
NX, NY, NZ, NC = 4, 8, 16, 2
MOST, ROWS, WIDTH, BLOCKS = 4, 16, 512, 64
FULL = 2
REST = MOST - FULL
CROWD = REST * NY
NEAR = (0, -1, 1, 2)


def nt(a, b):
    return lax.dot_general(a, b, (((1,), (1,)), ((), ())), preferred_element_type=jnp.float32)


def nn(a, b):
    return lax.dot_general(a, b, (((1,), (0,)), ((), ())), preferred_element_type=jnp.float32)


def kernel(
    cap, table, grads, left_stats, right_stats, moment, left_root, right_root,
    left_new, right_new, moment_new, direction,
    fresh, turned, blocks, stats, mine, sendx, recvx, sendy, recvy, sendq, recvq, crowd, sendr, recvr,
    low, full, roots, lefts, outbox, inbox, pair, tally,
    load_sem, save_sem, hello, xs, xr, ys, yr, qs, qr, ps, pr, rs, rr, us, ur, gs, gr, cs, cr, ns, nr, ls, lr, vs, vr, ts, tr,
):
    d, r = lax.axis_index("dp"), lax.axis_index("replica")
    x, y, z, c = d // NY, d % NY, r // NC, r % NC

    def at(dx=0, dy=0, dz=0, dc=0):
        return (((x + dx) % NX) * NY + (y + dy) % NY, ((z + dz) % NZ) * NC + (c + dc) % NC)

    def copy(src, dst, s, e, target):
        return pltpu.make_async_remote_copy(
            src_ref=src, dst_ref=dst, send_sem=s, recv_sem=e, device_id=target, device_id_type=MESH
        )

    def loop(start, stop, body):
        def step(i, carry):
            body(i)
            return carry

        lax.fori_loop(start, stop, step, 0)

    loads = [
        pltpu.make_async_copy(a, b, load_sem.at[i])
        for i, (a, b) in enumerate((
            (grads, blocks.at[pl.ds(0, BLOCKS)]),
            (left_root, mine.at[0]),
            (right_root, mine.at[1]),
            (moment, stats.at[2]),
            (left_stats, stats.at[0]),
            (right_stats, stats.at[1]),
        ))
    ]
    for load in loads:
        load.start()

    saves = [
        pltpu.make_async_copy(a, b, save_sem.at[i])
        for i, (a, b) in enumerate((
            (fresh.at[0], left_new),
            (fresh.at[1], right_new),
            (fresh.at[2], moment_new),
            (turned, direction),
        ))
    ]

    barrier = pltpu.get_barrier_semaphore()
    for i in range(1, NX):
        pl.semaphore_signal(barrier, inc=1, device_id=at(dx=i), device_id_type=MESH)
    for i in range(1, NY):
        pl.semaphore_signal(barrier, inc=1, device_id=at(dy=i), device_id_type=MESH)
    for i in (-2, -1, 1, 2):
        pl.semaphore_signal(barrier, inc=1, device_id=at(dz=i), device_id_type=MESH)
    pl.semaphore_signal(barrier, inc=1, device_id=at(dc=1), device_id_type=MESH)

    blocks[BLOCKS] = jnp.zeros((ROWS, WIDTH), jnp.bfloat16)
    crowd[CROWD] = jnp.zeros((ROWS, WIDTH), jnp.bfloat16)


    def greet(number, far):
        for i in (-far, far):
            pl.semaphore_signal(hello.at[number], inc=1, device_id=at(dz=i), device_id_type=MESH)


    def pick(k):
        def one(i):
            to, row = i // NY, i % NY
            sendx[k, to, row] = blocks[table[(((x + to) % NX) * NY + row) * FULL + k]]

        loop(0, NX * NY, one)

    def x_copy(k, i):
        return copy(sendx.at[k, i], recvx.at[k, i - 1], xs.at[k, i - 1], xr.at[k, i - 1], at(dx=i))

    def x_send(k):
        for i in range(1, NX):
            x_copy(k, i).start()

    def x_sum(k):
        for i in range(1, NX):
            x_copy(k, i).wait_recv()

        def one(row):
            total = sendx[k, 0, row].astype(jnp.float32)
            for i in range(NX - 1):
                total += recvx[k, i, row].astype(jnp.float32)
            sendy[k, row] = total.astype(jnp.bfloat16)

        loop(0, NY, one)

    def y_copy(k, i):
        return copy(
            sendy.at[k, (y + i) % NY], recvy.at[k, i - 1], ys.at[k, i - 1], yr.at[k, i - 1], at(dy=i)
        )

    def y_send(k):
        for i in range(1, NY):
            y_copy(k, i).start()

    def y_sum(k):
        for i in range(1, NY):
            y_copy(k, i).wait_recv()
        total = sendy[k, y].astype(jnp.float32)
        for i in range(NY - 1):
            total += recvy[k, i].astype(jnp.float32)
        low[k] = total.astype(jnp.bfloat16)


    def pick_rest():
        def one(i):
            to, row = i // cap, i % cap
            sendq[to, row] = blocks[table[BLOCKS + ((x + to) % NX) * CROWD + row]]

        loop(0, NX * cap, one)

    def q_copy(i):
        return copy(sendq.at[i], recvq.at[i - 1], qs.at[i - 1], qr.at[i - 1], at(dx=i))

    def q_sum():
        for i in range(1, NX):
            q_copy(i).wait_recv()

        def one(row):
            total = sendq[0, row].astype(jnp.float32)
            for i in range(NX - 1):
                total += recvq[i, row].astype(jnp.float32)
            crowd[row] = total.astype(jnp.bfloat16)

        loop(0, cap, one)

        def spread(i):
            to, row = i // REST, i % REST
            sendr[to, row] = crowd[table[BLOCKS + NX * CROWD + (x * NY + to) * REST + row]]

        loop(0, NY * REST, spread)

    def p_copy(i):
        return copy(sendr.at[(y + i) % NY], recvr.at[i - 1], ps.at[i - 1], pr.at[i - 1], at(dy=i))

    def p_sum():
        for i in range(1, NY):
            p_copy(i).wait_recv()
        total = sendr[y].astype(jnp.float32)
        for i in range(NY - 1):
            total += recvr[i].astype(jnp.float32)
        low[pl.ds(FULL, REST)] = total.astype(jnp.bfloat16)


    def root_copy(dz):
        return copy(mine.at[1, (z + dz) % MOST], roots.at[z, c], rs.at[dz], rr.at[dz], at(dz=dz))

    def root_relay():
        lane = roots.at[:, c]
        return copy(lane, lane, us.at[0], ur.at[0], at(dc=1))

    def g_copy(k, dz):
        return copy(low.at[k], full.at[z, c], gs.at[dz], gr.at[dz], at(dz=dz))

    def g_send(k):
        first = (k - z) % MOST
        for j in range(1, NZ // MOST):
            g_copy(k, first + j * MOST).start()

        @pl.when(first != 0)
        def _():
            g_copy(k, first).start()

        @pl.when(first == 0)
        def _():
            full[z, c] = low[k]

    def g_relay():
        lane = full.at[:, c]
        return copy(lane, lane, cs.at[0], cr.at[0], at(dc=1))

    def tally_copy(i):
        return copy(tally.at[0], tally.at[i], ts.at[i], tr.at[i], at(dz=i))

    def pair_copy():
        return copy(pair.at[0], pair.at[1], ts.at[0], tr.at[0], at(dc=1))

    def near_copy(part, i):
        return copy(outbox.at[i, part], inbox.at[i, part], ns.at[part, i - 1], nr.at[part, i - 1], at(dz=NEAR[i]))

    def left_copy(i):
        return copy(
            mine.at[0, (z - NEAR[i]) % MOST], lefts.at[i, c], ls.at[i - 1], lr.at[i - 1], at(dz=-NEAR[i])
        )

    def left_relay():
        piece = lefts.at[:, c]
        return copy(piece, piece, vs.at[0], vr.at[0], at(dc=1))

    loads[0].wait()
    pick_rest()
    pick(0)
    pl.semaphore_wait(barrier, NX - 1 + NY - 1 + 4 + NC - 1)
    greet(0, 2)
    for i in range(1, NX):
        q_copy(i).start()
    x_send(0)
    pick(1)
    loads[1].wait()
    loads[2].wait()
    lefts[0, c] = mine[0, z % MOST]
    for i in range(1, len(NEAR)):
        left_copy(i).start()
    roots[z, c] = mine[1, z % MOST]
    for dz in (1, 2, 14, 15):
        root_copy(dz).start()
    pl.semaphore_wait(hello.at[0], 2)
    greet(1, 4)
    for dz in (3, 4, 12, 13):
        root_copy(dz).start()
    q_sum()
    x_send(1)
    for i in range(1, NY):
        p_copy(i).start()
    pl.semaphore_wait(hello.at[1], 2)
    loop(5, 12, lambda dz: root_copy(dz).start())
    x_sum(0)
    y_send(0)
    for i in range(1, len(NEAR)):
        left_copy(i).wait()
    left_relay().start()
    p_sum()
    g_send(2)
    g_send(3)
    x_sum(1)
    y_send(1)
    y_sum(0)
    g_send(0)
    loop(1, NZ, lambda dz: root_copy(dz).wait_recv())
    root_relay().start()
    y_sum(1)
    g_send(1)

    lane = lax.broadcasted_iota(jnp.int32, (1, 128), 1)
    sums = jnp.zeros((1, 128), jnp.float32)
    for load in loads[3:]:
        load.wait()
    for k in range(MOST):
        wide = low[k].astype(jnp.float32)
        second = 0.95 * stats[2, k] + 0.05 * wide * wide
        fresh[2, k] = second
        adam = wide / (jnp.sqrt(second) + 1e-08)
        sums += jnp.where(lane == k, jnp.sum(adam * adam), 0.0)
    saves[2].start()
    pair[0] = sums
    pair_copy().start()
    for k in range(FULL):
        for i in range(1, NX):
            x_copy(k, i).wait_send()
        for i in range(1, NY):
            y_copy(k, i).wait_send()
    for i in range(1, NX):
        q_copy(i).wait_send()
    for i in range(1, NY):
        p_copy(i).wait_send()
    loop(1, NZ, lambda dz: root_copy(dz).wait_send())

    loop(1, NZ, lambda dz: g_copy(0, dz).wait_recv())
    g_relay().start()

    chosen = []
    for i in NEAR:
        base = ((z + i) % NZ) * (NC * ROWS) + c * ROWS
        rows = lax.broadcasted_iota(jnp.int32, (ROWS, WIDTH), 0) + base
        hit = lax.broadcasted_iota(jnp.int32, (ROWS, WIDTH), 1) == rows
        chosen.append(jnp.where(hit, 1.0, 0.0).astype(jnp.bfloat16))

    root_relay().wait()
    left_relay().wait()
    pair_copy().wait()
    g_relay().wait()

    many = len(NEAR) * ROWS
    block = full[...].reshape(WIDTH, WIDTH)
    right = roots[...].reshape(WIDTH, WIDTH)
    across = nt(jnp.concatenate([full[(z + i) % NZ, c] for i in NEAR] + chosen, axis=0), block)
    cols = across[many:].astype(jnp.bfloat16)

    def deliver(part, values):
        for i in range(len(NEAR)):
            box = inbox if i == 0 else outbox
            box[i, part] = values[i * ROWS:(i + 1) * ROWS].astype(jnp.bfloat16)
            if i > 0:
                near_copy(part, i).start()

    deliver(0, across[:many])
    down = nn(
        jnp.concatenate(
            [lefts[i, c] for i in range(len(NEAR))] + [lefts[i, 1 - c] for i in range(len(NEAR))] + [cols], axis=0
        ),
        block,
    )
    part = nn(down[:2 * many].astype(jnp.bfloat16), right)
    tally[0] = pair[0] + pair[1] + jnp.where(lane == MOST + z % MOST, jnp.sum(part * part), 0.0)
    loop(1, NZ, lambda i: tally_copy(i).start())
    deliver(1, down[2 * many:])
    deliver(2, part[:many])

    for j in range(2):
        for i in range(len(NEAR)):
            if i > 0:
                near_copy(j, i).wait()
            k = (z - NEAR[i]) % MOST
            fresh[j, k] = 0.9 * stats[j, k] + 0.1 * inbox[i, j].astype(jnp.float32)
        saves[j].start()

    for i in range(1, len(NEAR)):
        near_copy(2, i).wait()
    loop(1, NZ, lambda dz: g_copy(0, dz).wait_send())
    loop(1, NZ, lambda i: tally_copy(i).wait())
    totals = jnp.sum(tally[...], axis=0)
    entries = float(WIDTH * WIDTH)
    for i in range(len(NEAR)):
        k = (z - NEAR[i]) % MOST
        adam_total = jnp.sum(jnp.where(lane == k, totals, 0.0), axis=1, keepdims=True)
        shaped_total = jnp.sum(jnp.where(lane == MOST + k, totals, 0.0), axis=1, keepdims=True)
        ratio = jnp.sqrt(adam_total / entries) / jnp.sqrt(shaped_total / entries + 1e-06)
        turned[k] = (inbox[i, 2].astype(jnp.float32) * ratio).astype(jnp.bfloat16)
    saves[3].start()
    for save in saves:
        save.wait()


def write(*refs):
    sources, targets, held, into, out = refs[:4], refs[4:8], refs[8:12], refs[12], refs[13]
    loads = [pltpu.make_async_copy(sources[i], held[i], into.at[i]) for i in range(4)]
    saves = [pltpu.make_async_copy(held[i], targets[i], out.at[i]) for i in range(4)]
    for load in loads:
        load.start()
    for load, save in zip(loads, saves):
        load.wait()
        save.start()
    for save in saves:
        save.wait()


def on_device(grads, assignment, left_stats, right_stats, second_moment, left_root, right_root):
    owner = assignment[:, 0]
    numbers = jnp.arange(BLOCKS, dtype=jnp.int32)
    earlier = numbers[None, :] < numbers[:, None]
    same = (owner[:, None] == owner[None, :]) & earlier
    rank = jnp.sum(same.astype(jnp.int32), axis=1)
    late = rank >= FULL
    beside = (owner[:, None] // NY == owner[None, :] // NY) & late[None, :] & earlier
    place = jnp.sum(beside.astype(jnp.int32), axis=1)

    def lookup(key, value, size, empty):
        match = key[:, None] == jnp.arange(size, dtype=jnp.int32)[None, :]
        return empty + jnp.sum(jnp.where(match, value[:, None] - empty, 0), axis=0)

    owners = NX * NY
    table = jnp.concatenate([
        lookup(jnp.where(late, -1, owner * FULL + rank), numbers, owners * FULL, BLOCKS),
        lookup(jnp.where(late, owner // NY * CROWD + place, -1), numbers, NX * CROWD, BLOCKS),
        lookup(jnp.where(late, owner * REST + rank - FULL, -1), place, owners * REST, CROWD),
    ])
    lean = CROWD * 3 // 8
    fits = jnp.max(jnp.where(late, place, 0)) < lean
    operands = (table, grads[0], left_stats, right_stats, second_moment, left_root, right_root)
    return lax.cond(
        fits,
        lambda *given: step(lean, 0, *given),
        lambda *given: step(CROWD, 1, *given),
        *operands,
    )


def step(cap, number, *operands):
    wide = jax.ShapeDtypeStruct((MOST, ROWS, WIDTH), jnp.float32)
    narrow = jnp.bfloat16
    dma = pltpu.SemaphoreType.DMA
    tile = (ROWS, WIDTH)
    near = len(NEAR)

    def pair(*shape):
        return [dma(shape), dma(shape)]

    outs = [wide, wide, wide, jax.ShapeDtypeStruct((MOST, ROWS, WIDTH), narrow)]
    results = pl.pallas_call(
        functools.partial(kernel, cap),
        name="shampoo",
        out_shape=outs,
        in_specs=[pl.BlockSpec(memory_space=pltpu.SMEM)] + [pl.BlockSpec(memory_space=pl.ANY)] * 6,
        out_specs=[pl.BlockSpec(memory_space=pl.ANY)] * 4,
        scratch_shapes=[
            pltpu.VMEM((3, MOST, *tile), jnp.float32),
            pltpu.VMEM((MOST, *tile), narrow),
            pltpu.VMEM((BLOCKS + 1, *tile), narrow),
            pltpu.VMEM((3, MOST, *tile), jnp.float32),
            pltpu.VMEM((2, MOST, *tile), narrow),
            pltpu.VMEM((FULL, NX, NY, *tile), narrow),
            pltpu.VMEM((FULL, NX - 1, NY, *tile), narrow),
            pltpu.VMEM((FULL, NY, *tile), narrow),
            pltpu.VMEM((FULL, NY - 1, *tile), narrow),
            pltpu.VMEM((NX, cap, *tile), narrow),
            pltpu.VMEM((NX - 1, cap, *tile), narrow),
            pltpu.VMEM((CROWD + 1, *tile), narrow),
            pltpu.VMEM((NY, REST, *tile), narrow),
            pltpu.VMEM((NY - 1, REST, *tile), narrow),
            pltpu.VMEM((MOST, *tile), narrow),
            pltpu.VMEM((NZ, NC, *tile), narrow),
            pltpu.VMEM((NZ, NC, *tile), narrow),
            pltpu.VMEM((near, NC, *tile), narrow),
            pltpu.VMEM((near, 3, *tile), narrow),
            pltpu.VMEM((near, 3, *tile), narrow),
            pltpu.VMEM((NC, 1, 128), jnp.float32),
            pltpu.VMEM((NZ, 1, 128), jnp.float32),
            dma((6,)),
            dma((4,)),
            pltpu.SemaphoreType.REGULAR((2,)),
            *pair(FULL, NX - 1),
            *pair(FULL, NY - 1),
            *pair(NX - 1),
            *pair(NY - 1),
            *pair(NZ),
            *pair(1),
            *pair(NZ),
            *pair(1),
            *pair(3, near - 1),
            *pair(near - 1),
            *pair(1),
            *pair(NZ),
        ],
        compiler_params=pltpu.CompilerParams(
            collective_id=number, has_side_effects=True, vmem_limit_bytes=56 << 20
        ),
        cost_estimate=pl.CostEstimate(flops=800_000_000, bytes_accessed=2_400_000, transcendentals=70_000),
    )(*operands)
    return pl.pallas_call(
        write,
        name="write",
        out_shape=outs,
        in_specs=[pl.BlockSpec(memory_space=pl.ANY)] * 4,
        out_specs=[pl.BlockSpec(memory_space=pl.ANY)] * 4,
        scratch_shapes=[pltpu.VMEM(one.shape, one.dtype) for one in outs] + pair(4),
        compiler_params=pltpu.CompilerParams(vmem_limit_bytes=56 << 20),
    )(*results)


def solution(mesh):
    rows = P("dp", "replica", None)
    return jax.shard_map(
        on_device,
        mesh=mesh,
        in_specs=(P("dp", None, "replica", None), P(), rows, rows, rows, rows, rows),
        out_specs=(rows,) * 4,
        check_vma=False,
    )
```

```python
import functools

import jax
import jax.numpy as jnp
from jax import lax
from jax.experimental import pallas as pl
from jax.experimental.pallas import tpu as pltpu
from jax.sharding import PartitionSpec as P

MESH = pl.DeviceIdType.MESH
NX, NY, NZ, NC = 4, 8, 16, 2
MOST, ROWS, WIDTH, BLOCKS = 4, 16, 512, 64
FULL = 2
REST = MOST - FULL
CROWD = REST * NY
NEAR = (0, -1, 1, 2)


def nt(a, b):
    return lax.dot_general(a, b, (((1,), (1,)), ((), ())), preferred_element_type=jnp.float32)


def nn(a, b):
    return lax.dot_general(a, b, (((1,), (0,)), ((), ())), preferred_element_type=jnp.float32)


def kernel(
    cap, table, grads, left_stats, right_stats, moment, left_root, right_root,
    left_new, right_new, moment_new, direction,
    fresh, turned, blocks, stats, mine, sendx, recvx, sendy, recvy, sendq, recvq, crowd, sendr, recvr,
    low, full, roots, lefts, outbox, inbox, pair, tally,
    load_sem, save_sem, hello, xs, xr, ys, yr, qs, qr, ps, pr, rs, rr, us, ur, gs, gr, cs, cr, ns, nr, ls, lr, vs, vr, ts, tr,
):
    d, r = lax.axis_index("dp"), lax.axis_index("replica")
    x, y, z, c = d // NY, d % NY, r // NC, r % NC

    def at(dx=0, dy=0, dz=0, dc=0):
        return (((x + dx) % NX) * NY + (y + dy) % NY, ((z + dz) % NZ) * NC + (c + dc) % NC)

    def copy(src, dst, s, e, target):
        return pltpu.make_async_remote_copy(
            src_ref=src, dst_ref=dst, send_sem=s, recv_sem=e, device_id=target, device_id_type=MESH
        )

    def loop(start, stop, body):
        def step(i, carry):
            body(i)
            return carry

        lax.fori_loop(start, stop, step, 0)

    barrier = pltpu.get_barrier_semaphore()
    nearby = [at(dx=i) for i in (1, 2, 3)] + [at(dc=1)]
    nearby += [at(dy=i) for i in (-2, -1, 1, 2)] + [at(dz=i) for i in (-2, -1, 1, 2)]
    for device in nearby:
        pl.semaphore_signal(barrier, inc=1, device_id=device, device_id_type=MESH)

    loads = [
        pltpu.make_async_copy(a, b, load_sem.at[i])
        for i, (a, b) in enumerate((
            (grads, blocks.at[pl.ds(0, BLOCKS)]),
            (left_root, mine.at[0]),
            (right_root, mine.at[1]),
            (moment, stats.at[2]),
            (left_stats, stats.at[0]),
            (right_stats, stats.at[1]),
        ))
    ]
    for load in loads:
        load.start()

    saves = [
        pltpu.make_async_copy(a, b, save_sem.at[i])
        for i, (a, b) in enumerate((
            (fresh.at[0], left_new),
            (fresh.at[1], right_new),
            (fresh.at[2], moment_new),
            (turned, direction),
        ))
    ]

    blocks[BLOCKS] = jnp.zeros((ROWS, WIDTH), jnp.bfloat16)
    crowd[CROWD] = jnp.zeros((ROWS, WIDTH), jnp.bfloat16)


    def greet(number, *devices):
        for device in devices:
            pl.semaphore_signal(hello.at[number], inc=1, device_id=device, device_id_type=MESH)


    def pick(k):
        def one(i):
            to, row = i // NY, i % NY
            sendx[k, to, row] = blocks[table[(((x + to) % NX) * NY + row) * FULL + k]]

        loop(0, NX * NY, one)

    def x_copy(k, i):
        return copy(sendx.at[k, i], recvx.at[k, i - 1], xs.at[k, i - 1], xr.at[k, i - 1], at(dx=i))

    def x_send(k):
        for i in range(1, NX):
            x_copy(k, i).start()

    def x_sum(k):
        for i in range(1, NX):
            x_copy(k, i).wait_recv()

        def one(row):
            total = sendx[k, 0, row].astype(jnp.float32)
            for i in range(NX - 1):
                total += recvx[k, i, row].astype(jnp.float32)
            sendy[k, row] = total.astype(jnp.bfloat16)

        loop(0, NY, one)

    def y_copy(k, i):
        return copy(
            sendy.at[k, (y + i) % NY], recvy.at[k, i - 1], ys.at[k, i - 1], yr.at[k, i - 1], at(dy=i)
        )

    def y_send(k):
        for i in range(1, NY):
            y_copy(k, i).start()

    def y_sum(k):
        for i in range(1, NY):
            y_copy(k, i).wait_recv()
        total = sendy[k, y].astype(jnp.float32)
        for i in range(NY - 1):
            total += recvy[k, i].astype(jnp.float32)
        low[k] = total.astype(jnp.bfloat16)


    def pick_rest():
        def one(i):
            to, row = i // cap, i % cap
            sendq[to, row] = blocks[table[BLOCKS + ((x + to) % NX) * CROWD + row]]

        loop(0, NX * cap, one)

    def q_copy(i):
        return copy(sendq.at[i], recvq.at[i - 1], qs.at[i - 1], qr.at[i - 1], at(dx=i))

    def q_sum():
        for i in range(1, NX):
            q_copy(i).wait_recv()

        def one(row):
            total = sendq[0, row].astype(jnp.float32)
            for i in range(NX - 1):
                total += recvq[i, row].astype(jnp.float32)
            crowd[row] = total.astype(jnp.bfloat16)

        loop(0, cap, one)

        def spread(i):
            to, row = i // REST, i % REST
            sendr[to, row] = crowd[table[BLOCKS + NX * CROWD + (x * NY + to) * REST + row]]

        loop(0, NY * REST, spread)

    def p_copy(i):
        return copy(sendr.at[(y + i) % NY], recvr.at[i - 1], ps.at[i - 1], pr.at[i - 1], at(dy=i))

    def p_sum():
        for i in range(1, NY):
            p_copy(i).wait_recv()
        total = sendr[y].astype(jnp.float32)
        for i in range(NY - 1):
            total += recvr[i].astype(jnp.float32)
        low[pl.ds(FULL, REST)] = total.astype(jnp.bfloat16)


    def root_copy(dz):
        return copy(mine.at[1, (z + dz) % MOST], roots.at[z, c], rs.at[dz], rr.at[dz], at(dz=dz))

    def root_relay():
        lane = roots.at[:, c]
        return copy(lane, lane, us.at[0], ur.at[0], at(dc=1))

    def g_copy(k, dz):
        return copy(low.at[k], full.at[z, c], gs.at[dz], gr.at[dz], at(dz=dz))

    def g_send(k):
        first = (k - z) % MOST
        for j in range(1, NZ // MOST):
            g_copy(k, first + j * MOST).start()

        @pl.when(first != 0)
        def _():
            g_copy(k, first).start()

        @pl.when(first == 0)
        def _():
            full[z, c] = low[k]

    def g_relay():
        lane = full.at[:, c]
        return copy(lane, lane, cs.at[0], cr.at[0], at(dc=1))

    def tally_copy(i):
        return copy(tally.at[0], tally.at[i], ts.at[i], tr.at[i], at(dz=i))

    def pair_copy():
        return copy(pair.at[0], pair.at[1], ts.at[0], tr.at[0], at(dc=1))

    def near_copy(part, i):
        return copy(outbox.at[i, part], inbox.at[i, part], ns.at[part, i - 1], nr.at[part, i - 1], at(dz=NEAR[i]))

    def left_copy(i):
        return copy(
            mine.at[0, (z - NEAR[i]) % MOST], lefts.at[i, c], ls.at[i - 1], lr.at[i - 1], at(dz=-NEAR[i])
        )

    def left_relay():
        piece = lefts.at[:, c]
        return copy(piece, piece, vs.at[0], vr.at[0], at(dc=1))

    loads[0].wait()
    pick_rest()
    pl.semaphore_wait(barrier, len(nearby))
    greet(0, at(dy=-2), at(dy=2), at(dz=-2), at(dz=2))
    for i in range(1, NX):
        q_copy(i).start()
    pick(0)
    x_send(0)
    pick(1)
    loads[1].wait()
    loads[2].wait()
    lefts[0, c] = mine[0, z % MOST]
    for i in range(1, len(NEAR)):
        left_copy(i).start()
    roots[z, c] = mine[1, z % MOST]
    for dz in (1, 2, 14, 15):
        root_copy(dz).start()
    pl.semaphore_wait(hello.at[0], 4)
    greet(1, at(dz=-4), at(dz=4))
    for dz in (3, 4, 12, 13):
        root_copy(dz).start()
    q_sum()
    x_send(1)
    for i in range(1, NY):
        p_copy(i).start()
    pl.semaphore_wait(hello.at[1], 2)
    loop(5, 12, lambda dz: root_copy(dz).start())
    x_sum(0)
    y_send(0)
    for i in range(1, len(NEAR)):
        left_copy(i).wait()
    left_relay().start()
    p_sum()
    g_send(2)
    g_send(3)
    x_sum(1)
    y_send(1)
    y_sum(0)
    g_send(0)
    loop(1, NZ, lambda dz: root_copy(dz).wait_recv())
    root_relay().start()
    y_sum(1)
    g_send(1)

    lane = lax.broadcasted_iota(jnp.int32, (1, 128), 1)
    sums = jnp.zeros((1, 128), jnp.float32)
    for load in loads[3:]:
        load.wait()
    for k in range(MOST):
        wide = low[k].astype(jnp.float32)
        second = 0.95 * stats[2, k] + 0.05 * wide * wide
        fresh[2, k] = second
        adam = wide / (jnp.sqrt(second) + 1e-08)
        sums += jnp.where(lane == k, jnp.sum(adam * adam), 0.0)
    saves[2].start()
    pair[0] = sums
    pair_copy().start()
    for k in range(FULL):
        for i in range(1, NX):
            x_copy(k, i).wait_send()
        for i in range(1, NY):
            y_copy(k, i).wait_send()
    for i in range(1, NX):
        q_copy(i).wait_send()
    for i in range(1, NY):
        p_copy(i).wait_send()
    loop(1, NZ, lambda dz: root_copy(dz).wait_send())

    loop(1, NZ, lambda dz: g_copy(0, dz).wait_recv())
    g_relay().start()

    chosen = []
    for i in NEAR:
        base = ((z + i) % NZ) * (NC * ROWS) + c * ROWS
        rows = lax.broadcasted_iota(jnp.int32, (ROWS, WIDTH), 0) + base
        hit = lax.broadcasted_iota(jnp.int32, (ROWS, WIDTH), 1) == rows
        chosen.append(jnp.where(hit, 1.0, 0.0).astype(jnp.bfloat16))

    root_relay().wait()
    left_relay().wait()
    pair_copy().wait()
    g_relay().wait()

    many = len(NEAR) * ROWS
    block = full[...].reshape(WIDTH, WIDTH)
    right = roots[...].reshape(WIDTH, WIDTH)

    def deliver(part, values):
        for i in range(len(NEAR)):
            box = inbox if i == 0 else outbox
            box[i, part] = values[i * ROWS:(i + 1) * ROWS].astype(jnp.bfloat16)
            if i > 0:
                near_copy(part, i).start()

    lanes = [lefts[i, c] for i in range(len(NEAR))] + [lefts[i, 1 - c] for i in range(len(NEAR))]
    product = nn(jnp.concatenate(lanes, axis=0), block).astype(jnp.bfloat16)
    part = nn(product, right)
    tally[0] = pair[0] + pair[1] + jnp.where(lane == MOST + z % MOST, jnp.sum(part * part), 0.0)
    loop(1, NZ, lambda i: tally_copy(i).start())
    deliver(2, part[:many])
    across = nt(jnp.concatenate([full[(z + i) % NZ, c] for i in NEAR] + chosen, axis=0), block)
    deliver(0, across[:many])
    deliver(1, nn(across[many:].astype(jnp.bfloat16), block))

    for j in range(2):
        for i in range(len(NEAR)):
            if i > 0:
                near_copy(j, i).wait()
            k = (z - NEAR[i]) % MOST
            fresh[j, k] = 0.9 * stats[j, k] + 0.1 * inbox[i, j].astype(jnp.float32)
        saves[j].start()

    for i in range(1, len(NEAR)):
        near_copy(2, i).wait()
    loop(1, NZ, lambda dz: g_copy(0, dz).wait_send())
    loop(1, NZ, lambda i: tally_copy(i).wait())
    totals = jnp.sum(tally[...], axis=0)
    entries = float(WIDTH * WIDTH)
    for i in range(len(NEAR)):
        k = (z - NEAR[i]) % MOST
        adam_total = jnp.sum(jnp.where(lane == k, totals, 0.0), axis=1, keepdims=True)
        shaped_total = jnp.sum(jnp.where(lane == MOST + k, totals, 0.0), axis=1, keepdims=True)
        ratio = jnp.sqrt(adam_total / entries) / jnp.sqrt(shaped_total / entries + 1e-06)
        turned[k] = (inbox[i, 2].astype(jnp.float32) * ratio).astype(jnp.bfloat16)
    saves[3].start()
    for save in saves:
        save.wait()


def write(*refs):
    sources, targets, held, into, out = refs[:4], refs[4:8], refs[8:12], refs[12], refs[13]
    loads = [pltpu.make_async_copy(sources[i], held[i], into.at[i]) for i in range(4)]
    saves = [pltpu.make_async_copy(held[i], targets[i], out.at[i]) for i in range(4)]
    for load in loads:
        load.start()
    for load, save in zip(loads, saves):
        load.wait()
        save.start()
    for save in saves:
        save.wait()


def on_device(grads, assignment, left_stats, right_stats, second_moment, left_root, right_root):
    owner = assignment[:, 0]
    numbers = jnp.arange(BLOCKS, dtype=jnp.int32)
    earlier = numbers[None, :] < numbers[:, None]
    same = (owner[:, None] == owner[None, :]) & earlier
    rank = jnp.sum(same.astype(jnp.int32), axis=1)
    late = rank >= FULL
    beside = (owner[:, None] // NY == owner[None, :] // NY) & late[None, :] & earlier
    place = jnp.sum(beside.astype(jnp.int32), axis=1)

    def lookup(key, value, size, empty):
        match = key[:, None] == jnp.arange(size, dtype=jnp.int32)[None, :]
        return empty + jnp.sum(jnp.where(match, value[:, None] - empty, 0), axis=0)

    owners = NX * NY
    table = jnp.concatenate([
        lookup(jnp.where(late, -1, owner * FULL + rank), numbers, owners * FULL, BLOCKS),
        lookup(jnp.where(late, owner // NY * CROWD + place, -1), numbers, NX * CROWD, BLOCKS),
        lookup(jnp.where(late, owner * REST + rank - FULL, -1), place, owners * REST, CROWD),
    ])
    lean = CROWD * 3 // 8
    fits = jnp.max(jnp.where(late, place, 0)) < lean
    operands = (table, grads[0], left_stats, right_stats, second_moment, left_root, right_root)
    return lax.cond(
        fits,
        lambda *given: step(lean, 0, *given),
        lambda *given: step(CROWD, 1, *given),
        *operands,
    )


def step(cap, number, *operands):
    wide = jax.ShapeDtypeStruct((MOST, ROWS, WIDTH), jnp.float32)
    narrow = jnp.bfloat16
    dma = pltpu.SemaphoreType.DMA
    tile = (ROWS, WIDTH)
    near = len(NEAR)

    def pair(*shape):
        return [dma(shape), dma(shape)]

    outs = [wide, wide, wide, jax.ShapeDtypeStruct((MOST, ROWS, WIDTH), narrow)]
    results = pl.pallas_call(
        functools.partial(kernel, cap),
        name="shampoo",
        out_shape=outs,
        in_specs=[pl.BlockSpec(memory_space=pltpu.SMEM)] + [pl.BlockSpec(memory_space=pl.ANY)] * 6,
        out_specs=[pl.BlockSpec(memory_space=pl.ANY)] * 4,
        scratch_shapes=[
            pltpu.VMEM((3, MOST, *tile), jnp.float32),
            pltpu.VMEM((MOST, *tile), narrow),
            pltpu.VMEM((BLOCKS + 1, *tile), narrow),
            pltpu.VMEM((3, MOST, *tile), jnp.float32),
            pltpu.VMEM((2, MOST, *tile), narrow),
            pltpu.VMEM((FULL, NX, NY, *tile), narrow),
            pltpu.VMEM((FULL, NX - 1, NY, *tile), narrow),
            pltpu.VMEM((FULL, NY, *tile), narrow),
            pltpu.VMEM((FULL, NY - 1, *tile), narrow),
            pltpu.VMEM((NX, cap, *tile), narrow),
            pltpu.VMEM((NX - 1, cap, *tile), narrow),
            pltpu.VMEM((CROWD + 1, *tile), narrow),
            pltpu.VMEM((NY, REST, *tile), narrow),
            pltpu.VMEM((NY - 1, REST, *tile), narrow),
            pltpu.VMEM((MOST, *tile), narrow),
            pltpu.VMEM((NZ, NC, *tile), narrow),
            pltpu.VMEM((NZ, NC, *tile), narrow),
            pltpu.VMEM((near, NC, *tile), narrow),
            pltpu.VMEM((near, 3, *tile), narrow),
            pltpu.VMEM((near, 3, *tile), narrow),
            pltpu.VMEM((NC, 1, 128), jnp.float32),
            pltpu.VMEM((NZ, 1, 128), jnp.float32),
            dma((6,)),
            dma((4,)),
            pltpu.SemaphoreType.REGULAR((2,)),
            *pair(FULL, NX - 1),
            *pair(FULL, NY - 1),
            *pair(NX - 1),
            *pair(NY - 1),
            *pair(NZ),
            *pair(1),
            *pair(NZ),
            *pair(1),
            *pair(3, near - 1),
            *pair(near - 1),
            *pair(1),
            *pair(NZ),
        ],
        compiler_params=pltpu.CompilerParams(
            collective_id=number, has_side_effects=True, vmem_limit_bytes=56 << 20
        ),
        cost_estimate=pl.CostEstimate(flops=800_000_000, bytes_accessed=2_400_000, transcendentals=70_000),
    )(*operands)
    return pl.pallas_call(
        write,
        name="write",
        out_shape=outs,
        in_specs=[pl.BlockSpec(memory_space=pl.ANY)] * 4,
        out_specs=[pl.BlockSpec(memory_space=pl.ANY)] * 4,
        scratch_shapes=[pltpu.VMEM(one.shape, one.dtype) for one in outs] + pair(4),
        compiler_params=pltpu.CompilerParams(vmem_limit_bytes=56 << 20),
    )(*results)


def solution(mesh):
    rows = P("dp", "replica", None)
    return jax.shard_map(
        on_device,
        mesh=mesh,
        in_specs=(P("dp", None, "replica", None), P(), rows, rows, rows, rows, rows),
        out_specs=(rows,) * 4,
        check_vma=False,
    )
```

```python
import functools

import jax
import jax.numpy as jnp
from jax import lax
from jax.experimental import pallas as pl
from jax.experimental.pallas import tpu as pltpu
from jax.sharding import PartitionSpec as P

MESH = pl.DeviceIdType.MESH
NX, NY, NZ, NC = 4, 8, 16, 2
MOST, ROWS, WIDTH, BLOCKS = 4, 16, 512, 64
FULL = 2
REST = MOST - FULL
CROWD = REST * NY
NEAR = (0, -1, 1, 2)


def nt(a, b):
    return lax.dot_general(a, b, (((1,), (1,)), ((), ())), preferred_element_type=jnp.float32)


def nn(a, b):
    return lax.dot_general(a, b, (((1,), (0,)), ((), ())), preferred_element_type=jnp.float32)


def kernel(
    cap, table, grads, left_stats, right_stats, moment, left_root, right_root,
    left_new, right_new, moment_new, direction,
    fresh, turned, blocks, stats, mine, sendx, recvx, sendy, recvy, sendq, recvq, crowd, sendr, recvr,
    low, full, roots, lefts, outbox, inbox, pair, tally,
    load_sem, save_sem, hello, xs, xr, ys, yr, qs, qr, ps, pr, rs, rr, us, ur, gs, gr, cs, cr, ns, nr, ls, lr, vs, vr, ts, tr,
):
    d, r = lax.axis_index("dp"), lax.axis_index("replica")
    x, y, z, c = d // NY, d % NY, r // NC, r % NC

    def at(dx=0, dy=0, dz=0, dc=0):
        return (((x + dx) % NX) * NY + (y + dy) % NY, ((z + dz) % NZ) * NC + (c + dc) % NC)

    def copy(src, dst, s, e, target):
        return pltpu.make_async_remote_copy(
            src_ref=src, dst_ref=dst, send_sem=s, recv_sem=e, device_id=target, device_id_type=MESH
        )

    def loop(start, stop, body):
        def step(i, carry):
            body(i)
            return carry

        lax.fori_loop(start, stop, step, 0)

    barrier = pltpu.get_barrier_semaphore()
    nearby = [at(dx=i) for i in (1, 2, 3)] + [at(dc=1)]
    nearby += [at(dy=i) for i in (-2, -1, 1, 2)] + [at(dz=i) for i in (-2, -1, 1, 2)]
    for device in nearby:
        pl.semaphore_signal(barrier, inc=1, device_id=device, device_id_type=MESH)

    loads = [
        pltpu.make_async_copy(a, b, load_sem.at[i])
        for i, (a, b) in enumerate((
            (grads, blocks.at[pl.ds(0, BLOCKS)]),
            (left_root, mine.at[0]),
            (right_root, mine.at[1]),
            (moment, stats.at[2]),
            (left_stats, stats.at[0]),
            (right_stats, stats.at[1]),
        ))
    ]
    loads[0].start()

    saves = [
        pltpu.make_async_copy(a, b, save_sem.at[i])
        for i, (a, b) in enumerate((
            (fresh.at[0], left_new),
            (fresh.at[1], right_new),
            (fresh.at[2], moment_new),
            (turned, direction),
        ))
    ]

    blocks[BLOCKS] = jnp.zeros((ROWS, WIDTH), jnp.bfloat16)
    crowd[CROWD] = jnp.zeros((ROWS, WIDTH), jnp.bfloat16)


    def greet(number, *devices):
        for device in devices:
            pl.semaphore_signal(hello.at[number], inc=1, device_id=device, device_id_type=MESH)


    def pick(k):
        def one(i):
            to, row = i // NY, i % NY
            sendx[k, to, row] = blocks[table[(((x + to) % NX) * NY + row) * FULL + k]]

        loop(0, NX * NY, one)

    def x_copy(k, i):
        return copy(sendx.at[k, i], recvx.at[k, i - 1], xs.at[k, i - 1], xr.at[k, i - 1], at(dx=i))

    def x_send(k):
        for i in range(1, NX):
            x_copy(k, i).start()

    def x_sum(k):
        for i in range(1, NX):
            x_copy(k, i).wait_recv()

        def one(row):
            total = sendx[k, 0, row].astype(jnp.float32)
            for i in range(NX - 1):
                total += recvx[k, i, row].astype(jnp.float32)
            sendy[k, row] = total.astype(jnp.bfloat16)

        loop(0, NY, one)

    def y_copy(k, i):
        return copy(
            sendy.at[k, (y + i) % NY], recvy.at[k, i - 1], ys.at[k, i - 1], yr.at[k, i - 1], at(dy=i)
        )

    def y_send(k):
        for i in range(1, NY):
            y_copy(k, i).start()

    def y_sum(k):
        for i in range(1, NY):
            y_copy(k, i).wait_recv()
        total = sendy[k, y].astype(jnp.float32)
        for i in range(NY - 1):
            total += recvy[k, i].astype(jnp.float32)
        low[k] = total.astype(jnp.bfloat16)


    def pick_rest():
        def one(i):
            to, row = i // cap, i % cap
            sendq[to, row] = blocks[table[BLOCKS + ((x + to) % NX) * CROWD + row]]

        loop(0, NX * cap, one)

    def q_copy(i):
        return copy(sendq.at[i], recvq.at[i - 1], qs.at[i - 1], qr.at[i - 1], at(dx=i))

    def q_sum():
        for i in range(1, NX):
            q_copy(i).wait_recv()

        def one(row):
            total = sendq[0, row].astype(jnp.float32)
            for i in range(NX - 1):
                total += recvq[i, row].astype(jnp.float32)
            crowd[row] = total.astype(jnp.bfloat16)

        loop(0, cap, one)

        def spread(i):
            to, row = i // REST, i % REST
            sendr[to, row] = crowd[table[BLOCKS + NX * CROWD + (x * NY + to) * REST + row]]

        loop(0, NY * REST, spread)

    def p_copy(i):
        return copy(sendr.at[(y + i) % NY], recvr.at[i - 1], ps.at[i - 1], pr.at[i - 1], at(dy=i))

    def p_sum():
        for i in range(1, NY):
            p_copy(i).wait_recv()
        total = sendr[y].astype(jnp.float32)
        for i in range(NY - 1):
            total += recvr[i].astype(jnp.float32)
        low[pl.ds(FULL, REST)] = total.astype(jnp.bfloat16)


    def root_copy(dz):
        return copy(mine.at[1, (z + dz) % MOST], roots.at[z, c], rs.at[dz], rr.at[dz], at(dz=dz))

    def root_relay():
        lane = roots.at[:, c]
        return copy(lane, lane, us.at[0], ur.at[0], at(dc=1))

    def g_copy(k, dz):
        return copy(low.at[k], full.at[z, c], gs.at[dz], gr.at[dz], at(dz=dz))

    def g_send(k):
        first = (k - z) % MOST
        for j in range(1, NZ // MOST):
            g_copy(k, first + j * MOST).start()

        @pl.when(first != 0)
        def _():
            g_copy(k, first).start()

        @pl.when(first == 0)
        def _():
            full[z, c] = low[k]

    def g_relay():
        lane = full.at[:, c]
        return copy(lane, lane, cs.at[0], cr.at[0], at(dc=1))

    def tally_copy(i):
        return copy(tally.at[0], tally.at[i], ts.at[i], tr.at[i], at(dz=i))

    def pair_copy():
        return copy(pair.at[0], pair.at[1], ts.at[0], tr.at[0], at(dc=1))

    def near_copy(part, i):
        return copy(outbox.at[i, part], inbox.at[i, part], ns.at[part, i - 1], nr.at[part, i - 1], at(dz=NEAR[i]))

    def left_copy(i):
        return copy(
            mine.at[0, (z - NEAR[i]) % MOST], lefts.at[i, c], ls.at[i - 1], lr.at[i - 1], at(dz=-NEAR[i])
        )

    def left_relay():
        piece = lefts.at[:, c]
        return copy(piece, piece, vs.at[0], vr.at[0], at(dc=1))

    loads[0].wait()
    pick_rest()
    pl.semaphore_wait(barrier, len(nearby))
    greet(0, at(dy=-2), at(dy=2), at(dz=-2), at(dz=2))
    for i in range(1, NX):
        q_copy(i).start()
    for load in loads[1:]:
        load.start()
    pick(0)
    x_send(0)
    pick(1)
    loads[1].wait()
    loads[2].wait()
    lefts[0, c] = mine[0, z % MOST]
    for i in range(1, len(NEAR)):
        left_copy(i).start()
    roots[z, c] = mine[1, z % MOST]
    for dz in (1, 2, 14, 15):
        root_copy(dz).start()
    pl.semaphore_wait(hello.at[0], 4)
    greet(1, at(dz=-4), at(dz=4))
    for dz in (3, 4, 12, 13):
        root_copy(dz).start()
    q_sum()
    x_send(1)
    for i in range(1, NY):
        p_copy(i).start()
    pl.semaphore_wait(hello.at[1], 2)
    loop(5, 12, lambda dz: root_copy(dz).start())
    x_sum(0)
    y_send(0)
    for i in range(1, len(NEAR)):
        left_copy(i).wait()
    left_relay().start()
    p_sum()
    g_send(2)
    g_send(3)
    x_sum(1)
    y_send(1)
    y_sum(0)
    g_send(0)
    loop(1, NZ, lambda dz: root_copy(dz).wait_recv())
    root_relay().start()
    y_sum(1)
    g_send(1)

    lane = lax.broadcasted_iota(jnp.int32, (1, 128), 1)
    sums = jnp.zeros((1, 128), jnp.float32)
    for load in loads[3:]:
        load.wait()
    for k in range(MOST):
        wide = low[k].astype(jnp.float32)
        second = 0.95 * stats[2, k] + 0.05 * wide * wide
        fresh[2, k] = second
        adam = wide / (jnp.sqrt(second) + 1e-08)
        sums += jnp.where(lane == k, jnp.sum(adam * adam), 0.0)
    saves[2].start()
    pair[0] = sums
    pair_copy().start()
    for k in range(FULL):
        for i in range(1, NX):
            x_copy(k, i).wait_send()
        for i in range(1, NY):
            y_copy(k, i).wait_send()
    for i in range(1, NX):
        q_copy(i).wait_send()
    for i in range(1, NY):
        p_copy(i).wait_send()
    loop(1, NZ, lambda dz: root_copy(dz).wait_send())

    loop(1, NZ, lambda dz: g_copy(0, dz).wait_recv())
    g_relay().start()

    chosen = []
    for i in NEAR:
        base = ((z + i) % NZ) * (NC * ROWS) + c * ROWS
        rows = lax.broadcasted_iota(jnp.int32, (ROWS, WIDTH), 0) + base
        hit = lax.broadcasted_iota(jnp.int32, (ROWS, WIDTH), 1) == rows
        chosen.append(jnp.where(hit, 1.0, 0.0).astype(jnp.bfloat16))

    root_relay().wait()
    left_relay().wait()
    pair_copy().wait()
    g_relay().wait()

    many = len(NEAR) * ROWS
    block = full[...].reshape(WIDTH, WIDTH)
    right = roots[...].reshape(WIDTH, WIDTH)

    def deliver(part, values):
        for i in range(len(NEAR)):
            box = inbox if i == 0 else outbox
            box[i, part] = values[i * ROWS:(i + 1) * ROWS].astype(jnp.bfloat16)
            if i > 0:
                near_copy(part, i).start()

    lanes = [lefts[i, c] for i in range(len(NEAR))] + [lefts[i, 1 - c] for i in range(len(NEAR))]
    product = nn(jnp.concatenate(lanes, axis=0), block).astype(jnp.bfloat16)
    part = nn(product, right)
    tally[0] = pair[0] + pair[1] + jnp.where(lane == MOST + z % MOST, jnp.sum(part * part), 0.0)
    loop(1, NZ, lambda i: tally_copy(i).start())
    deliver(2, part[:many])
    across = nt(jnp.concatenate([full[(z + i) % NZ, c] for i in NEAR] + chosen, axis=0), block)
    deliver(0, across[:many])
    deliver(1, nn(across[many:].astype(jnp.bfloat16), block))

    for j in range(2):
        for i in range(len(NEAR)):
            if i > 0:
                near_copy(j, i).wait()
            k = (z - NEAR[i]) % MOST
            fresh[j, k] = 0.9 * stats[j, k] + 0.1 * inbox[i, j].astype(jnp.float32)
        saves[j].start()

    for i in range(1, len(NEAR)):
        near_copy(2, i).wait()
    loop(1, NZ, lambda dz: g_copy(0, dz).wait_send())
    loop(1, NZ, lambda i: tally_copy(i).wait())
    totals = jnp.sum(tally[...], axis=0)
    entries = float(WIDTH * WIDTH)
    for i in range(len(NEAR)):
        k = (z - NEAR[i]) % MOST
        adam_total = jnp.sum(jnp.where(lane == k, totals, 0.0), axis=1, keepdims=True)
        shaped_total = jnp.sum(jnp.where(lane == MOST + k, totals, 0.0), axis=1, keepdims=True)
        ratio = jnp.sqrt(adam_total / entries) / jnp.sqrt(shaped_total / entries + 1e-06)
        turned[k] = (inbox[i, 2].astype(jnp.float32) * ratio).astype(jnp.bfloat16)
    saves[3].start()
    for save in saves:
        save.wait()


def write(*refs):
    sources, targets, held, into, out = refs[:4], refs[4:8], refs[8:12], refs[12], refs[13]
    loads = [pltpu.make_async_copy(sources[i], held[i], into.at[i]) for i in range(4)]
    saves = [pltpu.make_async_copy(held[i], targets[i], out.at[i]) for i in range(4)]
    for load in loads:
        load.start()
    for load, save in zip(loads, saves):
        load.wait()
        save.start()
    for save in saves:
        save.wait()


def on_device(grads, assignment, left_stats, right_stats, second_moment, left_root, right_root):
    owner = assignment[:, 0]
    numbers = jnp.arange(BLOCKS, dtype=jnp.int32)
    earlier = numbers[None, :] < numbers[:, None]
    same = (owner[:, None] == owner[None, :]) & earlier
    rank = jnp.sum(same.astype(jnp.int32), axis=1)
    late = rank >= FULL
    beside = (owner[:, None] // NY == owner[None, :] // NY) & late[None, :] & earlier
    place = jnp.sum(beside.astype(jnp.int32), axis=1)

    def lookup(key, value, size, empty):
        match = key[:, None] == jnp.arange(size, dtype=jnp.int32)[None, :]
        return empty + jnp.sum(jnp.where(match, value[:, None] - empty, 0), axis=0)

    owners = NX * NY
    table = jnp.concatenate([
        lookup(jnp.where(late, -1, owner * FULL + rank), numbers, owners * FULL, BLOCKS),
        lookup(jnp.where(late, owner // NY * CROWD + place, -1), numbers, NX * CROWD, BLOCKS),
        lookup(jnp.where(late, owner * REST + rank - FULL, -1), place, owners * REST, CROWD),
    ])
    lean = CROWD * 3 // 8
    fits = jnp.max(jnp.where(late, place, 0)) < lean
    operands = (table, grads[0], left_stats, right_stats, second_moment, left_root, right_root)
    return lax.cond(
        fits,
        lambda *given: step(lean, 0, *given),
        lambda *given: step(CROWD, 1, *given),
        *operands,
    )


def step(cap, number, *operands):
    wide = jax.ShapeDtypeStruct((MOST, ROWS, WIDTH), jnp.float32)
    narrow = jnp.bfloat16
    dma = pltpu.SemaphoreType.DMA
    tile = (ROWS, WIDTH)
    near = len(NEAR)

    def pair(*shape):
        return [dma(shape), dma(shape)]

    outs = [wide, wide, wide, jax.ShapeDtypeStruct((MOST, ROWS, WIDTH), narrow)]
    results = pl.pallas_call(
        functools.partial(kernel, cap),
        name="shampoo",
        out_shape=outs,
        in_specs=[pl.BlockSpec(memory_space=pltpu.SMEM)] + [pl.BlockSpec(memory_space=pl.ANY)] * 6,
        out_specs=[pl.BlockSpec(memory_space=pl.ANY)] * 4,
        scratch_shapes=[
            pltpu.VMEM((3, MOST, *tile), jnp.float32),
            pltpu.VMEM((MOST, *tile), narrow),
            pltpu.VMEM((BLOCKS + 1, *tile), narrow),
            pltpu.VMEM((3, MOST, *tile), jnp.float32),
            pltpu.VMEM((2, MOST, *tile), narrow),
            pltpu.VMEM((FULL, NX, NY, *tile), narrow),
            pltpu.VMEM((FULL, NX - 1, NY, *tile), narrow),
            pltpu.VMEM((FULL, NY, *tile), narrow),
            pltpu.VMEM((FULL, NY - 1, *tile), narrow),
            pltpu.VMEM((NX, cap, *tile), narrow),
            pltpu.VMEM((NX - 1, cap, *tile), narrow),
            pltpu.VMEM((CROWD + 1, *tile), narrow),
            pltpu.VMEM((NY, REST, *tile), narrow),
            pltpu.VMEM((NY - 1, REST, *tile), narrow),
            pltpu.VMEM((MOST, *tile), narrow),
            pltpu.VMEM((NZ, NC, *tile), narrow),
            pltpu.VMEM((NZ, NC, *tile), narrow),
            pltpu.VMEM((near, NC, *tile), narrow),
            pltpu.VMEM((near, 3, *tile), narrow),
            pltpu.VMEM((near, 3, *tile), narrow),
            pltpu.VMEM((NC, 1, 128), jnp.float32),
            pltpu.VMEM((NZ, 1, 128), jnp.float32),
            dma((6,)),
            dma((4,)),
            pltpu.SemaphoreType.REGULAR((2,)),
            *pair(FULL, NX - 1),
            *pair(FULL, NY - 1),
            *pair(NX - 1),
            *pair(NY - 1),
            *pair(NZ),
            *pair(1),
            *pair(NZ),
            *pair(1),
            *pair(3, near - 1),
            *pair(near - 1),
            *pair(1),
            *pair(NZ),
        ],
        compiler_params=pltpu.CompilerParams(
            collective_id=number, has_side_effects=True, vmem_limit_bytes=56 << 20
        ),
        cost_estimate=pl.CostEstimate(flops=800_000_000, bytes_accessed=2_400_000, transcendentals=70_000),
    )(*operands)
    return pl.pallas_call(
        write,
        name="write",
        out_shape=outs,
        in_specs=[pl.BlockSpec(memory_space=pl.ANY)] * 4,
        out_specs=[pl.BlockSpec(memory_space=pl.ANY)] * 4,
        scratch_shapes=[pltpu.VMEM(one.shape, one.dtype) for one in outs] + pair(4),
        compiler_params=pltpu.CompilerParams(vmem_limit_bytes=56 << 20),
    )(*results)


def solution(mesh):
    rows = P("dp", "replica", None)
    return jax.shard_map(
        on_device,
        mesh=mesh,
        in_specs=(P("dp", None, "replica", None), P(), rows, rows, rows, rows, rows),
        out_specs=(rows,) * 4,
        check_vma=False,
    )
```
